256 devices in a mesh: section: 16 (over y, z_hi), ctx: 16 (over x, z_lo, core).
Axes of the slice: x: 4, y: 4, z: 8 (z_hi: 4, z_lo: 2; z = z_hi * 2 + z_lo), core: 2. Of those that a mesh axis runs over, the one named last changes fastest.
Arguments:
- queries: bfloat16 [16, 2048, 4096], P('section', 'ctx'), may hold values from -50 to 50, as said below
- keys: bfloat16 [16, 2048, 512], P('section', 'ctx'), may hold values from -5 to 5
- values: bfloat16 [16, 2048, 512], P('section', 'ctx'), may hold values from -12 to 12
- residual: bfloat16 [2048, 4096], P('ctx'), may hold values from -6 to 6
- span_map: int32 [16], replicated, may hold values from 0 to 15, as said below
Outputs:
- hidden_states: bfloat16 [16, 2048, 4096], P('section', 'ctx')
The draws below stay inside these ranges and needn't reach their ends.
Inputs may be any that keep to these rules, and one draw needn't show every extreme that they name: `queries`: queries of some rows may be large multiples of a visible key. `span_map`: each of the 16 spans appears exactly once.
All inputs are finite; a program needn't handle non-finite values.
Results may differ from the reference program's by a relative error of at most 0.008.
Values may be sent and summed in bfloat16 or wider, within the bound.
No kernel may reach another device: no remote copies, remote signals or barrier semaphores. Data moves between devices by JAX's collectives and lax.ppermute only.
A program may use at most 128 MiB of HBM per device.

```python
import math
import jax
import jax.numpy as jnp
from jax import lax

QUERY_HEADS = 32
KEY_VALUE_HEADS = 4
HEAD_SIZE = 128
TOK_DEV = 128
TRACE_TOKENS = 2048
LAYER_COUNT = 16
SPANS = 16


def span_layout(key):
    return jax.random.permutation(jax.random.fold_in(key, 21), SPANS).astype(jnp.int32)


def draw_span_map(key, part):
    common_factor = key
    return span_layout(common_factor)


def draw_keys(key, part):
    key = jax.random.fold_in(key, 3)
    final_output = jnp.clip(jax.random.normal(key, (LAYER_COUNT, TRACE_TOKENS, KEY_VALUE_HEADS * HEAD_SIZE), jnp.float32), -4.0, 4.0)
    return final_output.astype(jnp.bfloat16)


def draw_queries(key, part):
    key = jax.random.fold_in(key, 5)
    final_output = jnp.clip(1.5 * jax.random.normal(key, (LAYER_COUNT, TRACE_TOKENS, QUERY_HEADS * HEAD_SIZE), jnp.float32), -9.0, 9.0)
    return final_output.astype(jnp.bfloat16)


def levels(own_key, dims, shards, smallest, largest):
    gain, own = 1.0, jax.random.fold_in(own_key, 6)
    for dim, blocks in shards:
        heights = jnp.exp(jax.random.uniform(jax.random.fold_in(own, dim), (blocks,), jnp.float32, smallest / len(shards), largest / len(shards)))
        gain = gain * jnp.repeat(heights, dims[dim] // blocks).reshape([-1 if axis == dim else 1 for axis in range(len(dims))])
    return gain


def scatter_about(key, dims, deviation, bound, shards=(), held_as=jnp.bfloat16):
    factor_of = levels(key, dims, shards, -0.22, 0.18) if shards else 1.0
    values = jax.random.normal(key, dims, jnp.float32) * deviation * factor_of
    return jnp.minimum(jnp.maximum(values, -bound), bound).astype(held_as)


def setup_inputs(seed: int = 0) -> dict:
    key_list = jax.random.split(jax.random.key(seed), 6)
    queries = draw_queries(jax.random.fold_in(key_list[5], 71), 0)
    keys = draw_keys(jax.random.fold_in(key_list[5], 71), 0)
    values = scatter_about(key_list[2], (LAYER_COUNT, TRACE_TOKENS, KEY_VALUE_HEADS * HEAD_SIZE), 2.0, 12.0, ((0, 16), (1, 16)))
    residual = scatter_about(key_list[3], (TRACE_TOKENS, QUERY_HEADS * HEAD_SIZE), 1.0, 6.0, ((0, 16),))
    span_map = draw_span_map(jax.random.fold_in(key_list[5], 71), 0)
    return dict(queries=queries, keys=keys, values=values, residual=residual, span_map=span_map)


def token_positions(span_map):
    all_rows = jnp.arange(TRACE_TOKENS, dtype=jnp.int32)
    return (span_map[all_rows // TOK_DEV] * TOK_DEV + all_rows % TOK_DEV).astype(jnp.int32)

def layer_attention(layer_queries, layer_keys, layer_values, positions):
    query_groups = QUERY_HEADS // KEY_VALUE_HEADS
    query_head_rows = layer_queries.reshape(TRACE_TOKENS, KEY_VALUE_HEADS, query_groups, HEAD_SIZE).transpose(1, 2, 0, 3).reshape(QUERY_HEADS, TRACE_TOKENS, HEAD_SIZE)
    key_head_rows = jnp.repeat(layer_keys.reshape(TRACE_TOKENS, KEY_VALUE_HEADS, HEAD_SIZE).transpose(1, 0, 2), query_groups, axis=0)
    value_head_rows = jnp.repeat(layer_values.reshape(TRACE_TOKENS, KEY_VALUE_HEADS, HEAD_SIZE).transpose(1, 0, 2), query_groups, axis=0)
    visible = positions[None, :] <= positions[:, None]
    score_scale = 1.0 / math.sqrt(HEAD_SIZE)

    def one_head(operands):
        head_q, head_k, head_v = operands
        scores = jnp.dot(head_q, head_k.T, preferred_element_type=jnp.float32) * score_scale
        masked = jnp.where(visible, scores, jnp.float32(-1e+30))
        top_score = lax.optimization_barrier(jnp.max(masked, axis=1))
        weights = jnp.where(visible, jnp.exp(masked - top_score[:, None]), jnp.float32(0.0))
        totals = lax.optimization_barrier(jnp.sum(weights, axis=1))
        mixed = jnp.dot(weights.astype(jnp.bfloat16), head_v, preferred_element_type=jnp.float32)
        return mixed / totals[:, None]
    head_outputs = lax.map(one_head, (query_head_rows, key_head_rows, value_head_rows))
    return head_outputs.reshape(KEY_VALUE_HEADS, query_groups, TRACE_TOKENS, HEAD_SIZE).transpose(2, 0, 1, 3).reshape(TRACE_TOKENS, QUERY_HEADS * HEAD_SIZE)

def reference(queries, keys, values, residual, span_map):
    positions = token_positions(span_map)
    running = residual.astype(jnp.float32)
    stacked = []
    for layer in range(LAYER_COUNT):
        running = running + layer_attention(queries[layer], keys[layer], values[layer], positions)
        stacked.append(running.astype(jnp.bfloat16))
    return jnp.stack(stacked, axis=0)
```

```python
import functools
import math

import jax
import jax.numpy as jnp
from jax import lax
from jax.experimental import pallas as pl
from jax.experimental.pallas import tpu as pltpu
from jax.sharding import PartitionSpec as P

KEY_VALUE_HEADS = 4
GROUP = 8
HEAD_SIZE = 128
TOK = 128
SPANS = 16
LAYERS = 16
TRACE = SPANS * TOK
EXP2_SCALE = math.log2(math.e) / math.sqrt(HEAD_SIZE)
HIDDEN = -1e30
VMEM_LIMIT = 48 * 2**20


def attention_kernel(meta, q_ref, k_ref, v_ref, o_ref, keys, vals, eye, *, heads):
    @pl.when(pl.program_id(0) == 0)
    def _():
        key_row = lax.broadcasted_iota(jnp.int32, (TOK, TOK), 0)
        query_row = lax.broadcasted_iota(jnp.int32, (TOK, TOK), 1)
        eye[...] = jnp.where(key_row == query_row, 1.0, 0.0).astype(jnp.bfloat16)
        vals[:, HEAD_SIZE:] = jnp.ones((TRACE, HEAD_SIZE), jnp.bfloat16)
        for block in range(SPANS):
            ahead = (meta[block] - meta[SPANS]) * TOK + key_row - query_row
            keys[block * TOK : (block + 1) * TOK, HEAD_SIZE:] = jnp.where(
                ahead > 0, HIDDEN, 0.0
            ).astype(jnp.bfloat16)

    keys[:, :HEAD_SIZE] = k_ref[...].reshape(TRACE, HEAD_SIZE)
    vals[:, :HEAD_SIZE] = v_ref[...].reshape(TRACE, HEAD_SIZE)
    one_hot = eye[...]
    for tile in range(GROUP // heads):
        first = tile * heads
        q = jnp.concatenate(
            [
                jnp.concatenate(
                    [q_ref[:, h * HEAD_SIZE : (h + 1) * HEAD_SIZE], one_hot], axis=1
                )
                for h in range(first, first + heads)
            ],
            axis=0,
        )
        scores = lax.dot_general(
            q, keys[...], (((1,), (1,)), ((), ())), preferred_element_type=jnp.float32
        )
        peak = jnp.max(scores, axis=1, keepdims=True)
        weights = jnp.exp2((scores - peak) * EXP2_SCALE).astype(jnp.bfloat16)
        mixed = jnp.dot(weights, vals[...], preferred_element_type=jnp.float32)
        result = (mixed[:, :HEAD_SIZE] / mixed[:, HEAD_SIZE:]).astype(jnp.bfloat16)
        for i in range(heads):
            h = first + i
            o_ref[h // 2, :, (h % 2) * HEAD_SIZE : (h % 2 + 1) * HEAD_SIZE] = result[
                i * TOK : (i + 1) * TOK
            ]


def attention(queries, kv, meta, heads=2):
    width = GROUP * HEAD_SIZE
    return pl.pallas_call(
        functools.partial(attention_kernel, heads=heads),
        grid_spec=pltpu.PrefetchScalarGridSpec(
            num_scalar_prefetch=1,
            grid=(KEY_VALUE_HEADS,),
            in_specs=[
                pl.BlockSpec((TOK, width), lambda g, m: (0, g)),
                pl.BlockSpec((SPANS, TOK, HEAD_SIZE), lambda g, m: (0, 0, g)),
                pl.BlockSpec((SPANS, TOK, HEAD_SIZE), lambda g, m: (0, 0, KEY_VALUE_HEADS + g)),
            ],
            out_specs=pl.BlockSpec((4, TOK, 2 * HEAD_SIZE), lambda g, m: (g, 0, 0)),
            scratch_shapes=[
                pltpu.VMEM((TRACE, 2 * HEAD_SIZE), jnp.bfloat16),
                pltpu.VMEM((TRACE, 2 * HEAD_SIZE), jnp.bfloat16),
                pltpu.VMEM((TOK, TOK), jnp.bfloat16),
            ],
        ),
        out_shape=jax.ShapeDtypeStruct((LAYERS, TOK, 2 * HEAD_SIZE), jnp.bfloat16),
        compiler_params=pltpu.CompilerParams(vmem_limit_bytes=VMEM_LIMIT),
        name="attention",
    )(meta, queries, kv, kv)


def prefix_kernel(place, x_ref, residual_ref, o_ref):
    state = residual_ref[...].astype(jnp.float32)
    for layer in range(LAYERS):
        state = state + x_ref[layer].astype(jnp.float32)
        o_ref[layer] = state.astype(jnp.bfloat16)


def prefix(layers, residual, place):
    rows = 32
    width = 2 * HEAD_SIZE
    block = pl.BlockSpec((LAYERS, rows, width), lambda r, s: (0, r, 0))
    return pl.pallas_call(
        prefix_kernel,
        grid_spec=pltpu.PrefetchScalarGridSpec(
            num_scalar_prefetch=1,
            grid=(TOK // rows,),
            in_specs=[block, pl.BlockSpec((rows, width), lambda r, s: (r, s[0]))],
            out_specs=block,
        ),
        out_shape=jax.ShapeDtypeStruct((LAYERS, TOK, width), jnp.bfloat16),
        name="prefix",
    )(place, layers, residual)


def assemble_kernel(x_ref, o_ref):
    width = 2 * HEAD_SIZE
    for slab in range(LAYERS):
        o_ref[0, :, slab * width : (slab + 1) * width] = x_ref[slab]


def assemble(slabs):
    rows = 32
    width = LAYERS * 2 * HEAD_SIZE
    return pl.pallas_call(
        assemble_kernel,
        grid=(TOK // rows,),
        in_specs=[pl.BlockSpec((LAYERS, rows, 2 * HEAD_SIZE), lambda r: (0, r, 0))],
        out_specs=pl.BlockSpec((1, rows, width), lambda r: (0, r, 0)),
        out_shape=jax.ShapeDtypeStruct((1, TOK, width), jnp.bfloat16),
        name="assemble",
    )(slabs)


def body(queries, keys, values, residual, span_map):
    ctx = lax.axis_index("ctx")
    my_span = lax.dynamic_index_in_dim(span_map, ctx, 0, True)
    meta = jnp.concatenate([span_map, my_span])
    kv = lax.all_gather(jnp.concatenate([keys[0], values[0]], axis=1), "ctx")
    by_head = attention(queries[0], kv, meta)
    by_layer = lax.all_to_all(by_head, "section", 0, 0, tiled=True)
    summed = prefix(by_layer, residual, lax.axis_index("section")[None])
    mine = lax.all_to_all(summed, "section", 0, 0, tiled=True)
    return assemble(mine)


def solution(mesh):
    placed = (
        P("section", "ctx", None),
        P("section", "ctx", None),
        P("section", "ctx", None),
        P("ctx", None),
        P(),
    )
    return jax.shard_map(
        body, mesh=mesh, in_specs=placed, out_specs=P("section", "ctx", None), check_vma=False
    )
```

```python
import functools
import math

import jax
import jax.numpy as jnp
from jax import lax
from jax.experimental import pallas as pl
from jax.experimental.pallas import tpu as pltpu
from jax.sharding import PartitionSpec as P

KEY_VALUE_HEADS = 4
GROUP = 8
HEAD_SIZE = 128
TOK = 128
SPANS = 16
TRACE = SPANS * TOK
WIDTH = KEY_VALUE_HEADS * HEAD_SIZE
RING = 4
PAIR = 2 * HEAD_SIZE
EXP2_SCALE = math.log2(math.e) / math.sqrt(HEAD_SIZE)
HIDDEN = -1e30
VMEM_LIMIT = 40 * 2**20
CHUNKS = 2
PART = KEY_VALUE_HEADS // CHUNKS

UNITS = [(dx, dz, dc) for dc in range(2) for dz in range(2) for dx in range(4)]


def ctx_pairs(dx, dz, dc):
    pairs = []
    for i in range(SPANS):
        x, z, c = i // 4, i // 2 % 2, i % 2
        pairs.append((i, (x + dx) % 4 * 4 + (z ^ dz) * 2 + (c ^ dc)))
    return pairs


def ctx_move(unit, dx, dz, dc):
    return lax.ppermute(unit, "ctx", ctx_pairs(dx, dz, dc))


def turn_pairs(steps):
    return [(i, i // RING * RING + (i + steps) % RING) for i in range(RING * RING)]


def climb_pairs(steps):
    return [(i, i + RING * steps) for i in range(RING * (RING - steps))]


def join_kernel(k_ref, v_ref, o_ref):
    o_ref[:, :WIDTH] = k_ref[0]
    o_ref[:, WIDTH:] = v_ref[0]


def join(keys, values):
    return pl.pallas_call(
        join_kernel,
        out_shape=jax.ShapeDtypeStruct((TOK, 2 * WIDTH), jnp.bfloat16),
        name="join",
    )(keys, values)


def gather(keys, values):
    own = join(keys, values)
    held = {(0, 0, 0): own}
    held[0, 1, 0] = ctx_move(own, 0, 1, 0)
    for dx in (1, 3, 2):
        held[dx, 0, 0] = ctx_move(own, dx, 0, 0)
    for dx in (1, 3, 2):
        held[dx, 1, 0] = ctx_move(held[0, 1, 0], dx, 0, 0)
    for dz in range(2):
        for dx in range(4):
            held[dx, dz, 1] = ctx_move(held[dx, dz, 0], 0, 0, 1)
    return [held[unit] for unit in UNITS]


def attention_kernel(span_map, ctx, section, q_ref, *refs):
    k_refs, v_refs = refs[:SPANS], refs[SPANS : 2 * SPANS]
    o_refs = refs[2 * SPANS : 2 * SPANS + RING]
    keys, vals, eye = refs[2 * SPANS + RING :]

    @pl.when(pl.program_id(0) == 0)
    def _():
        key_row = lax.broadcasted_iota(jnp.int32, (TOK, TOK), 0)
        query_row = lax.broadcasted_iota(jnp.int32, (TOK, TOK), 1)
        eye[...] = jnp.where(key_row == query_row, 1.0, 0.0).astype(jnp.bfloat16)
        vals[:, HEAD_SIZE:] = jnp.ones((TRACE, HEAD_SIZE), jnp.bfloat16)
        me = ctx[0]
        my_span = span_map[me]
        x, z, c = me // 4, me // 2 % 2, me % 2
        for block, (dx, dz, dc) in enumerate(UNITS):
            source = (x + 4 - dx) % 4 * 4 + (z + dz) % 2 * 2 + (c + dc) % 2
            ahead = (span_map[source] - my_span) * TOK + key_row - query_row
            keys[block * TOK : (block + 1) * TOK, HEAD_SIZE:] = jnp.where(
                ahead > 0, HIDDEN, 0.0
            ).astype(jnp.bfloat16)

    for block in range(SPANS):
        rows = slice(block * TOK, (block + 1) * TOK)
        keys[rows, :HEAD_SIZE] = k_refs[block][...]
        vals[rows, :HEAD_SIZE] = v_refs[block][...]
    one_hot = eye[...]
    place = section[0] % RING
    for steps in range(RING):
        first = pl.multiple_of((place + steps) % RING * PAIR, PAIR)
        q = q_ref[:, pl.ds(first, PAIR)]
        q = jnp.concatenate(
            [
                jnp.concatenate([q[:, :HEAD_SIZE], one_hot], axis=1),
                jnp.concatenate([q[:, HEAD_SIZE:], one_hot], axis=1),
            ],
            axis=0,
        )
        scores = lax.dot_general(
            q, keys[...], (((1,), (1,)), ((), ())), preferred_element_type=jnp.float32
        )
        peak = jnp.max(scores, axis=1, keepdims=True)
        weights = jnp.exp2((scores - peak) * EXP2_SCALE).astype(jnp.bfloat16)
        mixed = jnp.dot(weights, vals[...], preferred_element_type=jnp.float32)
        result = (mixed[:, :HEAD_SIZE] / mixed[:, HEAD_SIZE:]).astype(jnp.bfloat16)
        o_refs[steps][:, :HEAD_SIZE] = result[:TOK]
        o_refs[steps][:, HEAD_SIZE:] = result[TOK:]


def attention(span_map, ctx, section, queries, units, chunk):
    base = chunk * PART
    slab = jax.ShapeDtypeStruct((TOK, PART * PAIR), jnp.bfloat16)
    return pl.pallas_call(
        attention_kernel,
        grid_spec=pltpu.PrefetchScalarGridSpec(
            num_scalar_prefetch=3,
            grid=(PART,),
            in_specs=[pl.BlockSpec((TOK, GROUP * HEAD_SIZE), lambda g, *_: (0, base + g))]
            + [pl.BlockSpec((TOK, HEAD_SIZE), lambda g, *_: (0, base + g))] * SPANS
            + [pl.BlockSpec((TOK, HEAD_SIZE), lambda g, *_: (0, KEY_VALUE_HEADS + base + g))]
            * SPANS,
            out_specs=[pl.BlockSpec((TOK, PAIR), lambda g, *_: (0, g))] * RING,
            scratch_shapes=[
                pltpu.VMEM((TRACE, PAIR), jnp.bfloat16),
                pltpu.VMEM((TRACE, PAIR), jnp.bfloat16),
                pltpu.VMEM((TOK, TOK), jnp.bfloat16),
            ],
        ),
        out_shape=[slab] * RING,
        compiler_params=pltpu.CompilerParams(vmem_limit_bytes=VMEM_LIMIT),
        cost_estimate=pl.CostEstimate(
            flops=PART * GROUP * TOK * TRACE * PAIR * 2 * 2,
            bytes_accessed=PART * (TRACE * PAIR + GROUP * TOK * PAIR) * 2,
            transcendentals=PART * GROUP * TOK * TRACE,
        ),
        name="attention",
    )(span_map, ctx, section, queries, *units, *units)


def total_kernel(a, b, c, d, o_ref):
    f32 = jnp.float32
    o_ref[...] = (
        a[...].astype(f32) + b[...].astype(f32) + (c[...].astype(f32) + d[...].astype(f32))
    ).astype(jnp.bfloat16)


def row_total(slabs):
    return pl.pallas_call(
        total_kernel,
        out_shape=jax.ShapeDtypeStruct((TOK, PART * PAIR), jnp.bfloat16),
        name="row_total",
    )(*slabs)


def prefix_kernel(chunk, section, residual_ref, *refs):
    slabs, below, outs = refs[:RING], refs[RING : 2 * RING - 1], refs[2 * RING - 1 : 3 * RING - 1]
    ordered, summed = refs[3 * RING - 1 :]
    place = section[0] % RING
    for steps in range(RING):
        ordered[(place + RING - steps) % RING] = slabs[steps][...]
    for part in range(PART):
        columns = slice(part * PAIR, (part + 1) * PAIR)
        first = (chunk * PART + part) * GROUP * HEAD_SIZE + place * PAIR
        state = residual_ref[:, pl.ds(pl.multiple_of(first, PAIR), PAIR)].astype(jnp.float32)
        for rows in below:
            state = state + rows[:, columns].astype(jnp.float32)
        for layer in range(RING):
            state = state + ordered[layer, :, columns].astype(jnp.float32)
            summed[layer, :, columns] = state.astype(jnp.bfloat16)
    for steps in range(RING):
        outs[steps][...] = summed[(place + steps) % RING]


def prefix(section, residual, slabs, below, chunk):
    slab = jax.ShapeDtypeStruct((TOK, PART * PAIR), jnp.bfloat16)
    whole = pl.BlockSpec(memory_space=pltpu.VMEM)
    return pl.pallas_call(
        functools.partial(prefix_kernel, chunk),
        in_specs=[pl.BlockSpec(memory_space=pltpu.SMEM)] + [whole] * (2 * RING),
        out_specs=[whole] * RING,
        out_shape=[slab] * RING,
        scratch_shapes=[
            pltpu.VMEM((RING, TOK, PART * PAIR), jnp.bfloat16),
            pltpu.VMEM((RING, TOK, PART * PAIR), jnp.bfloat16),
        ],
        name="prefix",
    )(section, residual, *slabs, *below)


def assemble_kernel(section, *refs):
    slabs, o_ref = refs[:-1], refs[-1]
    place = section[0] % RING
    for chunk in range(CHUNKS):
        for steps in range(RING):
            column = (place + RING - steps) % RING * PAIR
            for part in range(PART):
                first = (chunk * PART + part) * GROUP * HEAD_SIZE + column
                o_ref[0, :, pl.ds(pl.multiple_of(first, PAIR), PAIR)] = slabs[
                    chunk * RING + steps
                ][:, part * PAIR : (part + 1) * PAIR]


def assemble(section, slabs):
    whole = pl.BlockSpec(memory_space=pltpu.VMEM)
    width = KEY_VALUE_HEADS * GROUP * HEAD_SIZE
    return pl.pallas_call(
        assemble_kernel,
        in_specs=[pl.BlockSpec(memory_space=pltpu.SMEM)] + [whole] * len(slabs),
        out_specs=whole,
        out_shape=jax.ShapeDtypeStruct((1, TOK, width), jnp.bfloat16),
        name="assemble",
    )(section, *slabs)


def turn(slabs):
    return [slabs[0]] + [
        lax.ppermute(slabs[steps], "section", turn_pairs(steps)) for steps in range(1, RING)
    ]


def body(queries, keys, values, residual, span_map):
    ctx = lax.axis_index("ctx")[None]
    section = lax.axis_index("section")[None]
    units = gather(keys, values)
    finished = []
    for chunk in range(CHUNKS):
        slabs = turn(attention(span_map, ctx, section, queries[0], units, chunk))
        total = row_total(slabs)
        below = [lax.ppermute(total, "section", climb_pairs(s)) for s in range(1, RING)]
        finished += turn(prefix(section, residual, slabs, below, chunk))
    return assemble(section, finished)


def solution(mesh):
    placed = (
        P("section", "ctx", None),
        P("section", "ctx", None),
        P("section", "ctx", None),
        P("ctx", None),
        P(),
    )
    return jax.shard_map(
        body, mesh=mesh, in_specs=placed, out_specs=P("section", "ctx", None), check_vma=False
    )
```

```python
import functools
import math

import jax
import jax.numpy as jnp
from jax import lax
from jax.experimental import pallas as pl
from jax.experimental.pallas import tpu as pltpu
from jax.sharding import PartitionSpec as P

KEY_VALUE_HEADS = 4
GROUP = 8
HEAD_SIZE = 128
TOK = 128
SPANS = 16
TRACE = SPANS * TOK
WIDTH = KEY_VALUE_HEADS * HEAD_SIZE
LAYERS = 16
EXP2_SCALE = math.log2(math.e) / math.sqrt(HEAD_SIZE)
HIDDEN = -1e30
VMEM_LIMIT = 40 * 2**20
CHUNKS = 2
PART = KEY_VALUE_HEADS // CHUNKS

UNITS = [(dx, dz, dc) for dc in range(2) for dz in range(2) for dx in range(4)]


def ctx_pairs(dx, dz, dc):
    pairs = []
    for i in range(SPANS):
        x, z, c = i // 4, i // 2 % 2, i % 2
        pairs.append((i, (x + dx) % 4 * 4 + (z ^ dz) * 2 + (c ^ dc)))
    return pairs


def ctx_move(unit, dx, dz, dc):
    return lax.ppermute(unit, "ctx", ctx_pairs(dx, dz, dc))


def join_kernel(k_ref, v_ref, o_ref, sems):
    copies = [
        pltpu.make_async_copy(k_ref.at[0], o_ref.at[:, :WIDTH], sems.at[0]),
        pltpu.make_async_copy(v_ref.at[0], o_ref.at[:, WIDTH:], sems.at[1]),
    ]
    for copy in copies:
        copy.start()
    for copy in copies:
        copy.wait()


def join(keys, values):
    return pl.pallas_call(
        join_kernel,
        in_specs=[pl.BlockSpec(memory_space=pltpu.HBM)] * 2,
        out_specs=pl.BlockSpec(memory_space=pltpu.VMEM),
        out_shape=jax.ShapeDtypeStruct((TOK, 2 * WIDTH), jnp.bfloat16),
        scratch_shapes=[pltpu.SemaphoreType.DMA((2,))],
        name="join",
    )(keys, values)


def gather(keys, values):
    held = {(0, 0, 0): join(keys, values)}
    for dx, dz, source in (
        (0, 1, (0, 0, 0)),
        (1, 0, (0, 0, 0)),
        (3, 0, (0, 0, 0)),
        (0, 1, (1, 0, 0)),
        (1, 0, (1, 0, 0)),
        (3, 0, (0, 1, 0)),
        (0, 1, (2, 0, 0)),
    ):
        target = ((source[0] + dx) % 4, source[1] ^ dz, 0)
        held[target] = ctx_move(held[source], dx, dz, 0)
    for dz in range(2):
        for dx in range(4):
            held[dx, dz, 1] = ctx_move(held[dx, dz, 0], 0, 0, 1)
    return [held[unit] for unit in UNITS]


def attention_kernel(base, span_map, ctx, q_hbm, *refs):
    units, o_ref = refs[:SPANS], refs[SPANS]
    q_ref, keys, vals, eye, sems = refs[SPANS + 1 :]
    head_columns = pl.ds(base * GROUP * HEAD_SIZE, PART * GROUP * HEAD_SIZE)
    copies = [[pltpu.make_async_copy(q_hbm.at[:, head_columns], q_ref, sems.at[PART, 0])]]
    for part in range(PART):
        group = []
        for block in range(SPANS):
            for side, held in enumerate((keys, vals)):
                first = side * WIDTH + (base + part) * HEAD_SIZE
                group.append(
                    pltpu.make_async_copy(
                        units[block].at[:, pl.ds(first, HEAD_SIZE)],
                        held.at[part, pl.ds(block * TOK, TOK), pl.ds(0, HEAD_SIZE)],
                        sems.at[part, 2 * block + side],
                    )
                )
        copies.append(group)
    for group in copies:
        for copy in group:
            copy.start()

    key_row = lax.broadcasted_iota(jnp.int32, (TOK, TOK), 0)
    query_row = lax.broadcasted_iota(jnp.int32, (TOK, TOK), 1)
    eye[...] = jnp.where(key_row == query_row, 1.0, 0.0).astype(jnp.bfloat16)
    me = ctx[0]
    my_span = span_map[me]
    x, z, c = me // 4, me // 2 % 2, me % 2
    for block, (dx, dz, dc) in enumerate(UNITS):
        source = (x + 4 - dx) % 4 * 4 + (z + dz) % 2 * 2 + (c + dc) % 2
        ahead = (span_map[source] - my_span) * TOK + key_row - query_row
        mask = jnp.where(ahead > 0, HIDDEN, 0.0).astype(jnp.bfloat16)
        for part in range(PART):
            keys[part, block * TOK : (block + 1) * TOK, HEAD_SIZE:] = mask
    for part in range(PART):
        vals[part, :, HEAD_SIZE:] = jnp.ones((TRACE, HEAD_SIZE), jnp.bfloat16)

    copies[0][0].wait()
    one_hot = eye[...]
    for part in range(PART):
        for copy in copies[1 + part]:
            copy.wait()
        for head in range(part * GROUP, (part + 1) * GROUP, 2):
            q = q_ref[:, head * HEAD_SIZE : (head + 2) * HEAD_SIZE]
            q = jnp.concatenate(
                [
                    jnp.concatenate([q[:, :HEAD_SIZE], one_hot], axis=1),
                    jnp.concatenate([q[:, HEAD_SIZE:], one_hot], axis=1),
                ],
                axis=0,
            )
            scores = lax.dot_general(
                q, keys[part], (((1,), (1,)), ((), ())), preferred_element_type=jnp.float32
            )
            peak = jnp.max(scores, axis=1, keepdims=True)
            weights = jnp.exp2((scores - peak) * EXP2_SCALE).astype(jnp.bfloat16)
            mixed = jnp.dot(weights, vals[part], preferred_element_type=jnp.float32)
            result = (mixed[:, :HEAD_SIZE] / mixed[:, HEAD_SIZE:]).astype(jnp.bfloat16)
            o_ref[head] = result[:TOK]
            o_ref[head + 1] = result[TOK:]


def attention(span_map, ctx, queries, units, chunk):
    smem = pl.BlockSpec(memory_space=pltpu.SMEM)
    return pl.pallas_call(
        functools.partial(attention_kernel, chunk * PART),
        in_specs=[smem, smem, pl.BlockSpec(memory_space=pltpu.HBM)]
        + [pl.BlockSpec(memory_space=pltpu.HBM)] * SPANS,
        out_specs=pl.BlockSpec(memory_space=pltpu.VMEM),
        out_shape=jax.ShapeDtypeStruct((LAYERS, TOK, HEAD_SIZE), jnp.bfloat16),
        scratch_shapes=[
            pltpu.VMEM((TOK, PART * GROUP * HEAD_SIZE), jnp.bfloat16),
            pltpu.VMEM((PART, TRACE, 2 * HEAD_SIZE), jnp.bfloat16),
            pltpu.VMEM((PART, TRACE, 2 * HEAD_SIZE), jnp.bfloat16),
            pltpu.VMEM((TOK, TOK), jnp.bfloat16),
            pltpu.SemaphoreType.DMA((PART + 1, 2 * SPANS)),
        ],
        compiler_params=pltpu.CompilerParams(vmem_limit_bytes=VMEM_LIMIT),
        cost_estimate=pl.CostEstimate(
            flops=PART * GROUP * TOK * TRACE * 2 * HEAD_SIZE * 2 * 2,
            bytes_accessed=PART * (TRACE + GROUP * TOK) * 2 * HEAD_SIZE * 2,
            transcendentals=PART * GROUP * TOK * TRACE,
        ),
        name="attention",
    )(span_map, ctx, pltpu.with_memory_space_constraint(queries, pltpu.HBM), *[pltpu.with_memory_space_constraint(u, pltpu.HBM) for u in units])


def prefix_kernel(chunk, section, residual_hbm, x_ref, o_ref, first, sem):
    column = pl.multiple_of((chunk * LAYERS + section[0]) * HEAD_SIZE, HEAD_SIZE)
    copy = pltpu.make_async_copy(residual_hbm.at[:, pl.ds(column, HEAD_SIZE)], first, sem)
    copy.start()
    copy.wait()
    state = first[...].astype(jnp.float32)
    for layer in range(LAYERS):
        state = state + x_ref[layer].astype(jnp.float32)
        o_ref[layer] = state.astype(jnp.bfloat16)


def prefix(section, residual, layers, chunk):
    whole = pl.BlockSpec(memory_space=pltpu.VMEM)
    return pl.pallas_call(
        functools.partial(prefix_kernel, chunk),
        in_specs=[
            pl.BlockSpec(memory_space=pltpu.SMEM),
            pl.BlockSpec(memory_space=pltpu.HBM),
            whole,
        ],
        out_specs=whole,
        out_shape=jax.ShapeDtypeStruct((LAYERS, TOK, HEAD_SIZE), jnp.bfloat16),
        scratch_shapes=[pltpu.VMEM((TOK, HEAD_SIZE), jnp.bfloat16), pltpu.SemaphoreType.DMA(())],
        name="prefix",
    )(section, residual, layers)


def assemble_kernel(*refs):
    slabs, o_ref, sems = refs[:CHUNKS], refs[CHUNKS], refs[CHUNKS + 1]
    copies = []
    for chunk in range(CHUNKS):
        for slab in range(LAYERS):
            head = chunk * LAYERS + slab
            copies.append(
                pltpu.make_async_copy(
                    slabs[chunk].at[slab],
                    o_ref.at[0, :, pl.ds(head * HEAD_SIZE, HEAD_SIZE)],
                    sems.at[head],
                )
            )
    for copy in copies:
        copy.start()
    for copy in copies:
        copy.wait()


def assemble(slabs):
    heads = KEY_VALUE_HEADS * GROUP
    return pl.pallas_call(
        assemble_kernel,
        in_specs=[pl.BlockSpec(memory_space=pl.ANY)] * CHUNKS,
        out_specs=pl.BlockSpec(memory_space=pltpu.HBM),
        out_shape=jax.ShapeDtypeStruct((1, TOK, heads * HEAD_SIZE), jnp.bfloat16),
        scratch_shapes=[pltpu.SemaphoreType.DMA((heads,))],
        name="assemble",
    )(*slabs)


def body(queries, keys, values, residual, span_map):
    ctx = lax.axis_index("ctx")[None]
    section = lax.axis_index("section")[None]
    units = gather(keys, values)
    finished = []
    for chunk in range(CHUNKS):
        by_head = attention(span_map, ctx, queries[0], units, chunk)
        by_layer = lax.all_to_all(by_head, "section", 0, 0, tiled=True)
        summed = prefix(section, residual, by_layer, chunk)
        finished.append(lax.all_to_all(summed, "section", 0, 0, tiled=True))
    return assemble(finished)


def solution(mesh):
    placed = (
        P("section", "ctx", None),
        P("section", "ctx", None),
        P("section", "ctx", None),
        P("ctx", None),
        P(),
    )
    return jax.shard_map(
        body, mesh=mesh, in_specs=placed, out_specs=P("section", "ctx", None), check_vma=False
    )
```

```python
import functools
import math

import jax
import jax.numpy as jnp
from jax import lax
from jax.experimental import pallas as pl
from jax.experimental.pallas import tpu as pltpu
from jax.sharding import PartitionSpec as P

KEY_VALUE_HEADS = 4
GROUP = 8
HEAD_SIZE = 128
TOK = 128
SPANS = 16
TRACE = SPANS * TOK
WIDTH = KEY_VALUE_HEADS * HEAD_SIZE
RING = 4
PAIR = 2 * HEAD_SIZE
EXP2_SCALE = math.log2(math.e) / math.sqrt(HEAD_SIZE)
HIDDEN = -1e30
VMEM_LIMIT = 20 * 2**20
CHUNKS = 2
PART = KEY_VALUE_HEADS // CHUNKS

UNITS = [(dx, dz, dc) for dc in range(2) for dz in range(2) for dx in range(4)]


def ctx_pairs(dx, dz, dc):
    pairs = []
    for i in range(SPANS):
        x, z, c = i // 4, i // 2 % 2, i % 2
        pairs.append((i, (x + dx) % 4 * 4 + (z ^ dz) * 2 + (c ^ dc)))
    return pairs


def ctx_move(unit, dx, dz, dc):
    return lax.ppermute(unit, "ctx", ctx_pairs(dx, dz, dc))


def turn_pairs(steps):
    return [(i, i // RING * RING + (i + steps) % RING) for i in range(RING * RING)]


def climb_pairs(steps):
    return [(i, i + RING * steps) for i in range(RING * (RING - steps))]


def pinned(x):
    return pltpu.with_memory_space_constraint(x, pltpu.HBM)


def join_kernel(k_ref, v_ref, o_ref):
    o_ref[:, :WIDTH] = k_ref[0]
    o_ref[:, WIDTH:] = v_ref[0]


def join(keys, values):
    return pl.pallas_call(
        join_kernel,
        out_shape=jax.ShapeDtypeStruct((TOK, 2 * WIDTH), jnp.bfloat16),
        compiler_params=pltpu.CompilerParams(vmem_limit_bytes=2 * 2**20),
        name="join",
    )(keys, values)


def gather(keys, values):
    held = {(0, 0, 0): join(keys, values)}
    for dx, dz, source in (
        (0, 1, (0, 0, 0)),
        (1, 0, (0, 0, 0)),
        (3, 0, (0, 0, 0)),
        (0, 1, (1, 0, 0)),
        (1, 0, (1, 0, 0)),
        (3, 0, (0, 1, 0)),
        (0, 1, (2, 0, 0)),
    ):
        target = ((source[0] + dx) % 4, source[1] ^ dz, 0)
        held[target] = ctx_move(held[source], dx, dz, 0)
    for dz in range(2):
        for dx in range(4):
            held[dx, dz, 1] = ctx_move(held[dx, dz, 0], 0, 0, 1)
    return [held[unit] for unit in UNITS]


def attention_kernel(span_map, ctx, section, q_ref, *refs):
    k_refs, v_refs = refs[:SPANS], refs[SPANS : 2 * SPANS]
    o_refs = refs[2 * SPANS : 2 * SPANS + RING]
    keys, vals, eye = refs[2 * SPANS + RING :]

    @pl.when(pl.program_id(0) == 0)
    def _():
        key_row = lax.broadcasted_iota(jnp.int32, (TOK, TOK), 0)
        query_row = lax.broadcasted_iota(jnp.int32, (TOK, TOK), 1)
        eye[...] = jnp.where(key_row == query_row, 1.0, 0.0).astype(jnp.bfloat16)
        vals[:, HEAD_SIZE:] = jnp.ones((TRACE, HEAD_SIZE), jnp.bfloat16)
        me = ctx[0]
        my_span = span_map[me]
        x, z, c = me // 4, me // 2 % 2, me % 2
        for block, (dx, dz, dc) in enumerate(UNITS):
            source = (x + 4 - dx) % 4 * 4 + (z + dz) % 2 * 2 + (c + dc) % 2
            ahead = (span_map[source] - my_span) * TOK + key_row - query_row
            keys[block * TOK : (block + 1) * TOK, HEAD_SIZE:] = jnp.where(
                ahead > 0, HIDDEN, 0.0
            ).astype(jnp.bfloat16)

    for block in range(SPANS):
        rows = slice(block * TOK, (block + 1) * TOK)
        keys[rows, :HEAD_SIZE] = k_refs[block][...]
        vals[rows, :HEAD_SIZE] = v_refs[block][...]
    one_hot = eye[...]
    place = section[0] % RING
    for steps in range(RING):
        first = pl.multiple_of((place + steps) % RING * PAIR, PAIR)
        q = q_ref[:, pl.ds(first, PAIR)]
        q = jnp.concatenate(
            [
                jnp.concatenate([q[:, :HEAD_SIZE], one_hot], axis=1),
                jnp.concatenate([q[:, HEAD_SIZE:], one_hot], axis=1),
            ],
            axis=0,
        )
        scores = lax.dot_general(
            q, keys[...], (((1,), (1,)), ((), ())), preferred_element_type=jnp.float32
        )
        peak = jnp.max(scores, axis=1, keepdims=True)
        weights = jnp.exp2((scores - peak) * EXP2_SCALE).astype(jnp.bfloat16)
        mixed = jnp.dot(weights, vals[...], preferred_element_type=jnp.float32)
        result = (mixed[:, :HEAD_SIZE] / mixed[:, HEAD_SIZE:]).astype(jnp.bfloat16)
        o_refs[steps][:, :HEAD_SIZE] = result[:TOK]
        o_refs[steps][:, HEAD_SIZE:] = result[TOK:]


def attention(span_map, ctx, section, queries, units, chunk):
    base = chunk * PART
    slab = jax.ShapeDtypeStruct((TOK, PART * PAIR), jnp.bfloat16)
    return pl.pallas_call(
        attention_kernel,
        grid_spec=pltpu.PrefetchScalarGridSpec(
            num_scalar_prefetch=3,
            grid=(PART,),
            in_specs=[pl.BlockSpec((TOK, GROUP * HEAD_SIZE), lambda g, *_: (0, base + g))]
            + [pl.BlockSpec((TOK, HEAD_SIZE), lambda g, *_: (0, base + g))] * SPANS
            + [pl.BlockSpec((TOK, HEAD_SIZE), lambda g, *_: (0, KEY_VALUE_HEADS + base + g))]
            * SPANS,
            out_specs=[pl.BlockSpec((TOK, PAIR), lambda g, *_: (0, g))] * RING,
            scratch_shapes=[
                pltpu.VMEM((TRACE, PAIR), jnp.bfloat16),
                pltpu.VMEM((TRACE, PAIR), jnp.bfloat16),
                pltpu.VMEM((TOK, TOK), jnp.bfloat16),
            ],
        ),
        out_shape=[slab] * RING,
        compiler_params=pltpu.CompilerParams(vmem_limit_bytes=VMEM_LIMIT),
        cost_estimate=pl.CostEstimate(
            flops=PART * GROUP * TOK * TRACE * PAIR * 2 * 2,
            bytes_accessed=PART * (TRACE * PAIR + GROUP * TOK * PAIR) * 2,
            transcendentals=PART * GROUP * TOK * TRACE,
        ),
        name="attention",
    )(
        pinned(span_map), ctx, section, pinned(queries), *units, *units
    )


def total_kernel(a, b, c, d, o_ref):
    f32 = jnp.float32
    o_ref[...] = (
        a[...].astype(f32) + b[...].astype(f32) + (c[...].astype(f32) + d[...].astype(f32))
    ).astype(jnp.bfloat16)


def row_total(slabs):
    return pl.pallas_call(
        total_kernel,
        in_specs=[pl.BlockSpec(memory_space=pltpu.VMEM)] * RING,
        out_specs=pl.BlockSpec(memory_space=pltpu.VMEM),
        out_shape=jax.ShapeDtypeStruct((TOK, PART * PAIR), jnp.bfloat16),
        compiler_params=pltpu.CompilerParams(vmem_limit_bytes=4 * 2**20),
        name="row_total",
    )(*slabs)


def prefix_kernel(chunk, section, residual_ref, *refs):
    slabs, below, outs = refs[:RING], refs[RING : 2 * RING - 1], refs[2 * RING - 1 : 3 * RING - 1]
    ordered, summed = refs[3 * RING - 1 :]
    place = section[0] % RING
    for steps in range(RING):
        ordered[(place + RING - steps) % RING] = slabs[steps][...]
    for part in range(PART):
        columns = slice(part * PAIR, (part + 1) * PAIR)
        first = (chunk * PART + part) * GROUP * HEAD_SIZE + place * PAIR
        state = residual_ref[:, pl.ds(pl.multiple_of(first, PAIR), PAIR)].astype(jnp.float32)
        for rows in below:
            state = state + rows[:, columns].astype(jnp.float32)
        for layer in range(RING):
            state = state + ordered[layer, :, columns].astype(jnp.float32)
            summed[layer, :, columns] = state.astype(jnp.bfloat16)
    for steps in range(RING):
        outs[steps][...] = summed[(place + steps) % RING]


def prefix(section, residual, slabs, below, chunk):
    slab = jax.ShapeDtypeStruct((TOK, PART * PAIR), jnp.bfloat16)
    whole = pl.BlockSpec(memory_space=pltpu.VMEM)
    return pl.pallas_call(
        functools.partial(prefix_kernel, chunk),
        in_specs=[pl.BlockSpec(memory_space=pltpu.SMEM)] + [whole] * (2 * RING),
        out_specs=[whole] * RING,
        out_shape=[slab] * RING,
        scratch_shapes=[
            pltpu.VMEM((RING, TOK, PART * PAIR), jnp.bfloat16),
            pltpu.VMEM((RING, TOK, PART * PAIR), jnp.bfloat16),
        ],
        compiler_params=pltpu.CompilerParams(vmem_limit_bytes=8 * 2**20),
        name="prefix",
    )(section, residual, *slabs, *below)


def assemble_kernel(section, *refs):
    slabs, o_ref = refs[:-1], refs[-1]
    place = section[0] % RING
    for chunk in range(CHUNKS):
        for steps in range(RING):
            column = (place + RING - steps) % RING * PAIR
            for part in range(PART):
                first = (chunk * PART + part) * GROUP * HEAD_SIZE + column
                o_ref[0, :, pl.ds(pl.multiple_of(first, PAIR), PAIR)] = slabs[
                    chunk * RING + steps
                ][:, part * PAIR : (part + 1) * PAIR]


def assemble(section, slabs):
    whole = pl.BlockSpec(memory_space=pltpu.VMEM)
    width = KEY_VALUE_HEADS * GROUP * HEAD_SIZE
    return pl.pallas_call(
        assemble_kernel,
        in_specs=[pl.BlockSpec(memory_space=pltpu.SMEM)] + [whole] * len(slabs),
        out_specs=whole,
        out_shape=jax.ShapeDtypeStruct((1, TOK, width), jnp.bfloat16),
        compiler_params=pltpu.CompilerParams(vmem_limit_bytes=8 * 2**20),
        name="assemble",
    )(section, *slabs)


def turn(slabs):
    return [slabs[0]] + [
        lax.ppermute(slabs[steps], "section", turn_pairs(steps)) for steps in range(1, RING)
    ]


def body(queries, keys, values, residual, span_map):
    ctx = lax.axis_index("ctx")[None]
    section = lax.axis_index("section")[None]
    units = gather(keys, values)
    finished = []
    for chunk in range(CHUNKS):
        slabs = turn(attention(span_map, ctx, section, queries[0], units, chunk))
        total = row_total(slabs)
        below = [lax.ppermute(total, "section", climb_pairs(s)) for s in range(1, RING)]
        finished += turn(prefix(section, residual, slabs, below, chunk))
    return assemble(section, finished)


def solution(mesh):
    placed = (
        P("section", "ctx", None),
        P("section", "ctx", None),
        P("section", "ctx", None),
        P("ctx", None),
        P(),
    )
    return jax.shard_map(
        body, mesh=mesh, in_specs=placed, out_specs=P("section", "ctx", None), check_vma=False
    )
```

```python
import functools
import math

import jax
import jax.numpy as jnp
from jax import lax
from jax.experimental import pallas as pl
from jax.experimental.pallas import tpu as pltpu
from jax.sharding import PartitionSpec as P

KEY_VALUE_HEADS = 4
GROUP = 8
HEAD_SIZE = 128
TOK = 128
SPANS = 16
TRACE = SPANS * TOK
WIDTH = KEY_VALUE_HEADS * HEAD_SIZE
RING = 4
PAIR = 2 * HEAD_SIZE
EXP2_SCALE = math.log2(math.e) / math.sqrt(HEAD_SIZE)
HIDDEN = -1e30
VMEM_LIMIT = 20 * 2**20
CHUNKS = 2
PART = KEY_VALUE_HEADS // CHUNKS

UNITS = [(dx, dz, dc) for dc in range(2) for dz in range(2) for dx in range(4)]


def ctx_pairs(dx, dz, dc):
    pairs = []
    for i in range(SPANS):
        x, z, c = i // 4, i // 2 % 2, i % 2
        pairs.append((i, (x + dx) % 4 * 4 + (z ^ dz) * 2 + (c ^ dc)))
    return pairs


def ctx_move(unit, dx, dz, dc):
    return lax.ppermute(unit, "ctx", ctx_pairs(dx, dz, dc))


def turn_pairs(steps):
    return [(i, i // RING * RING + (i + steps) % RING) for i in range(RING * RING)]


def climb_pairs(steps):
    return [(i, (i + RING * steps) % (RING * RING)) for i in range(RING * RING)]


def pinned(x):
    return pltpu.with_memory_space_constraint(x, pltpu.HBM)


def join_kernel(k_ref, v_ref, o_ref):
    o_ref[:, :WIDTH] = k_ref[0]
    o_ref[:, WIDTH:] = v_ref[0]


def join(keys, values):
    return pl.pallas_call(
        join_kernel,
        out_shape=jax.ShapeDtypeStruct((TOK, 2 * WIDTH), jnp.bfloat16),
        compiler_params=pltpu.CompilerParams(vmem_limit_bytes=2 * 2**20),
        name="join",
    )(keys, values)


def gather(keys, values):
    held = {(0, 0, 0): join(keys, values)}
    for dx, dz, source in (
        (0, 1, (0, 0, 0)),
        (1, 0, (0, 0, 0)),
        (3, 0, (0, 0, 0)),
        (0, 1, (1, 0, 0)),
        (1, 0, (1, 0, 0)),
        (3, 0, (0, 1, 0)),
        (0, 1, (2, 0, 0)),
    ):
        target = ((source[0] + dx) % 4, source[1] ^ dz, 0)
        held[target] = ctx_move(held[source], dx, dz, 0)
    for dz in range(2):
        for dx in range(4):
            held[dx, dz, 1] = ctx_move(held[dx, dz, 0], 0, 0, 1)
    return [held[unit] for unit in UNITS]


def attention_kernel(span_map, ctx, section, q_ref, *refs):
    k_refs, v_refs = refs[:SPANS], refs[SPANS : 2 * SPANS]
    o_refs = refs[2 * SPANS : 2 * SPANS + RING]
    keys, vals, eye = refs[2 * SPANS + RING :]

    @pl.when(pl.program_id(0) == 0)
    def _():
        key_row = lax.broadcasted_iota(jnp.int32, (TOK, TOK), 0)
        query_row = lax.broadcasted_iota(jnp.int32, (TOK, TOK), 1)
        eye[...] = jnp.where(key_row == query_row, 1.0, 0.0).astype(jnp.bfloat16)
        vals[:, HEAD_SIZE:] = jnp.ones((TRACE, HEAD_SIZE), jnp.bfloat16)
        me = ctx[0]
        my_span = span_map[me]
        x, z, c = me // 4, me // 2 % 2, me % 2
        for block, (dx, dz, dc) in enumerate(UNITS):
            source = (x + 4 - dx) % 4 * 4 + (z + dz) % 2 * 2 + (c + dc) % 2
            ahead = (span_map[source] - my_span) * TOK + key_row - query_row
            keys[block * TOK : (block + 1) * TOK, HEAD_SIZE:] = jnp.where(
                ahead > 0, HIDDEN, 0.0
            ).astype(jnp.bfloat16)

    for block in range(SPANS):
        rows = slice(block * TOK, (block + 1) * TOK)
        keys[rows, :HEAD_SIZE] = k_refs[block][...]
        vals[rows, :HEAD_SIZE] = v_refs[block][...]
    one_hot = eye[...]
    place = section[0] % RING
    for steps in range(RING):
        first = pl.multiple_of((place + steps) % RING * PAIR, PAIR)
        q = q_ref[:, pl.ds(first, PAIR)]
        q = jnp.concatenate(
            [
                jnp.concatenate([q[:, :HEAD_SIZE], one_hot], axis=1),
                jnp.concatenate([q[:, HEAD_SIZE:], one_hot], axis=1),
            ],
            axis=0,
        )
        scores = lax.dot_general(
            q, keys[...], (((1,), (1,)), ((), ())), preferred_element_type=jnp.float32
        )
        peak = jnp.max(scores, axis=1, keepdims=True)
        weights = jnp.exp2((scores - peak) * EXP2_SCALE).astype(jnp.bfloat16)
        mixed = jnp.dot(weights, vals[...], preferred_element_type=jnp.float32)
        result = (mixed[:, :HEAD_SIZE] / mixed[:, HEAD_SIZE:]).astype(jnp.bfloat16)
        o_refs[steps][:, :HEAD_SIZE] = result[:TOK]
        o_refs[steps][:, HEAD_SIZE:] = result[TOK:]


def attention(span_map, ctx, section, queries, units, chunk):
    base = chunk * PART
    slab = jax.ShapeDtypeStruct((TOK, PART * PAIR), jnp.bfloat16)
    return pl.pallas_call(
        attention_kernel,
        grid_spec=pltpu.PrefetchScalarGridSpec(
            num_scalar_prefetch=3,
            grid=(PART,),
            in_specs=[pl.BlockSpec((TOK, GROUP * HEAD_SIZE), lambda g, *_: (0, base + g))]
            + [pl.BlockSpec((TOK, HEAD_SIZE), lambda g, *_: (0, base + g))] * SPANS
            + [pl.BlockSpec((TOK, HEAD_SIZE), lambda g, *_: (0, KEY_VALUE_HEADS + base + g))]
            * SPANS,
            out_specs=[pl.BlockSpec((TOK, PAIR), lambda g, *_: (0, g))] * RING,
            scratch_shapes=[
                pltpu.VMEM((TRACE, PAIR), jnp.bfloat16),
                pltpu.VMEM((TRACE, PAIR), jnp.bfloat16),
                pltpu.VMEM((TOK, TOK), jnp.bfloat16),
            ],
        ),
        out_shape=[slab] * RING,
        compiler_params=pltpu.CompilerParams(vmem_limit_bytes=VMEM_LIMIT),
        cost_estimate=pl.CostEstimate(
            flops=PART * GROUP * TOK * TRACE * PAIR * 2 * 2,
            bytes_accessed=PART * (TRACE * PAIR + GROUP * TOK * PAIR) * 2,
            transcendentals=PART * GROUP * TOK * TRACE,
        ),
        name="attention",
    )(
        pinned(span_map), ctx, section, pinned(queries), *units, *units
    )


def total_kernel(a, b, c, d, o_ref):
    f32 = jnp.float32
    o_ref[...] = (
        a[...].astype(f32) + b[...].astype(f32) + (c[...].astype(f32) + d[...].astype(f32))
    ).astype(jnp.bfloat16)


def row_total(slabs):
    return pl.pallas_call(
        total_kernel,
        in_specs=[pl.BlockSpec(memory_space=pltpu.VMEM)] * RING,
        out_specs=pl.BlockSpec(memory_space=pltpu.VMEM),
        out_shape=jax.ShapeDtypeStruct((TOK, PART * PAIR), jnp.bfloat16),
        compiler_params=pltpu.CompilerParams(vmem_limit_bytes=4 * 2**20),
        name="row_total",
    )(*slabs)


def prefix_kernel(chunk, section, residual_ref, *refs):
    slabs, below, outs = refs[:RING], refs[RING : 2 * RING - 1], refs[2 * RING - 1 : 3 * RING - 1]
    ordered, summed = refs[3 * RING - 1 :]
    place, row = section[0] % RING, section[0] // RING
    for steps in range(RING):
        ordered[(place + RING - steps) % RING] = slabs[steps][...]
    for part in range(PART):
        columns = slice(part * PAIR, (part + 1) * PAIR)
        first = (chunk * PART + part) * GROUP * HEAD_SIZE + place * PAIR
        state = residual_ref[:, pl.ds(pl.multiple_of(first, PAIR), PAIR)].astype(jnp.float32)
        for steps, rows in enumerate(below, 1):
            earlier = rows[:, columns].astype(jnp.float32)
            state = state + jnp.where(row >= steps, earlier, 0.0)
        for layer in range(RING):
            state = state + ordered[layer, :, columns].astype(jnp.float32)
            summed[layer, :, columns] = state.astype(jnp.bfloat16)
    for steps in range(RING):
        outs[steps][...] = summed[(place + steps) % RING]


def prefix(section, residual, slabs, below, chunk):
    slab = jax.ShapeDtypeStruct((TOK, PART * PAIR), jnp.bfloat16)
    whole = pl.BlockSpec(memory_space=pltpu.VMEM)
    return pl.pallas_call(
        functools.partial(prefix_kernel, chunk),
        in_specs=[pl.BlockSpec(memory_space=pltpu.SMEM)] + [whole] * (2 * RING),
        out_specs=[whole] * RING,
        out_shape=[slab] * RING,
        scratch_shapes=[
            pltpu.VMEM((RING, TOK, PART * PAIR), jnp.bfloat16),
            pltpu.VMEM((RING, TOK, PART * PAIR), jnp.bfloat16),
        ],
        compiler_params=pltpu.CompilerParams(vmem_limit_bytes=8 * 2**20),
        name="prefix",
    )(section, residual, *slabs, *below)


def assemble_kernel(section, *refs):
    slabs, o_ref = refs[:-1], refs[-1]
    place = section[0] % RING
    for chunk in range(CHUNKS):
        for steps in range(RING):
            column = (place + RING - steps) % RING * PAIR
            for part in range(PART):
                first = (chunk * PART + part) * GROUP * HEAD_SIZE + column
                o_ref[0, :, pl.ds(pl.multiple_of(first, PAIR), PAIR)] = slabs[
                    chunk * RING + steps
                ][:, part * PAIR : (part + 1) * PAIR]


def assemble(section, slabs):
    whole = pl.BlockSpec(memory_space=pltpu.VMEM)
    width = KEY_VALUE_HEADS * GROUP * HEAD_SIZE
    return pl.pallas_call(
        assemble_kernel,
        in_specs=[pl.BlockSpec(memory_space=pltpu.SMEM)] + [whole] * len(slabs),
        out_specs=whole,
        out_shape=jax.ShapeDtypeStruct((1, TOK, width), jnp.bfloat16),
        compiler_params=pltpu.CompilerParams(vmem_limit_bytes=8 * 2**20),
        name="assemble",
    )(section, *slabs)


def turn(slabs):
    return [slabs[0]] + [
        lax.ppermute(slabs[steps], "section", turn_pairs(steps)) for steps in range(1, RING)
    ]


def body(queries, keys, values, residual, span_map):
    ctx = lax.axis_index("ctx")[None]
    section = lax.axis_index("section")[None]
    units = gather(keys, values)
    slabs = [
        turn(attention(span_map, ctx, section, queries[0], units, chunk))
        for chunk in range(CHUNKS)
    ]
    finished, sums = [], None
    for chunk in range(CHUNKS):
        total = row_total(slabs[chunk])
        if sums is not None:
            total, *sums = lax.optimization_barrier((total, *sums))
            finished += turn(sums)
        below = [lax.ppermute(total, "section", climb_pairs(s)) for s in range(1, RING)]
        sums = prefix(section, residual, slabs[chunk], below, chunk)
    finished += turn(sums)
    return assemble(section, finished)


def solution(mesh):
    placed = (
        P("section", "ctx", None),
        P("section", "ctx", None),
        P("section", "ctx", None),
        P("ctx", None),
        P(),
    )
    return jax.shard_map(
        body, mesh=mesh, in_specs=placed, out_specs=P("section", "ctx", None), check_vma=False
    )
```

```python
import functools
import math

import jax
import jax.numpy as jnp
from jax import lax
from jax.experimental import pallas as pl
from jax.experimental.pallas import tpu as pltpu
from jax.sharding import PartitionSpec as P

KEY_VALUE_HEADS = 4
GROUP = 8
HEAD_SIZE = 128
TOK = 128
SPANS = 16
WIDTH = KEY_VALUE_HEADS * HEAD_SIZE
RING = 4
PAIR = 2 * HEAD_SIZE
EXP2_SCALE = math.log2(math.e) / math.sqrt(HEAD_SIZE)
HIDDEN = -1e30
VMEM_LIMIT = 20 * 2**20
CHUNKS = 2
PART = KEY_VALUE_HEADS // CHUNKS

EARLY = [(0, 0, 0), (0, 0, 1), (0, 1, 0), (1, 0, 0), (3, 0, 0), (0, 1, 1)]
MIDDLE = [(1, 0, 1), (3, 0, 1), (2, 0, 0), (1, 1, 0), (3, 1, 0), (2, 0, 1)]
LATE = [(1, 1, 1), (3, 1, 1), (2, 1, 0), (2, 1, 1)]


def ctx_pairs(dx, dz, dc):
    pairs = []
    for i in range(SPANS):
        x, z, c = i // 4, i // 2 % 2, i % 2
        pairs.append((i, (x + dx) % 4 * 4 + (z ^ dz) * 2 + (c ^ dc)))
    return pairs


def ctx_move(unit, dx, dz, dc):
    return lax.ppermute(unit, "ctx", ctx_pairs(dx, dz, dc))


def turn_pairs(steps):
    return [(i, i // RING * RING + (i + steps) % RING) for i in range(RING * RING)]


def climb_pairs(steps):
    return [(i, (i + RING * steps) % (RING * RING)) for i in range(RING * RING)]


def pinned(x):
    return pltpu.with_memory_space_constraint(x, pltpu.HBM)


def join_kernel(k_ref, v_ref, o_ref):
    o_ref[:, :WIDTH] = k_ref[0]
    o_ref[:, WIDTH:] = v_ref[0]


def join(keys, values):
    return pl.pallas_call(
        join_kernel,
        out_shape=jax.ShapeDtypeStruct((TOK, 2 * WIDTH), jnp.bfloat16),
        compiler_params=pltpu.CompilerParams(vmem_limit_bytes=2 * 2**20),
        name="join",
    )(keys, values)


def gather(keys, values):
    held = {(0, 0, 0): join(keys, values)}
    for dx, dz, source in (
        (0, 1, (0, 0, 0)),
        (1, 0, (0, 0, 0)),
        (3, 0, (0, 0, 0)),
        (0, 1, (1, 0, 0)),
        (1, 0, (1, 0, 0)),
        (3, 0, (0, 1, 0)),
        (0, 1, (2, 0, 0)),
    ):
        target = ((source[0] + dx) % 4, source[1] ^ dz, 0)
        held[target] = ctx_move(held[source], dx, dz, 0)
    for dz in range(2):
        for dx in range(4):
            held[dx, dz, 1] = ctx_move(held[dx, dz, 0], 0, 0, 1)
    return held


def attention_kernel(units, base, first, last, span_map, ctx, section, q_ref, *refs):
    count = len(units)
    k_refs, v_refs, refs = refs[:count], refs[count : 2 * count], refs[2 * count :]
    if not first:
        (sums_in, peak_in), refs = refs[:2], refs[2:]
    if last:
        o_refs, refs = refs[:RING], refs[RING:]
    else:
        (sums_out, peak_out), refs = refs[:2], refs[2:]
    keys, vals, eye = refs
    group = base + pl.program_id(0)

    @pl.when(pl.program_id(0) == 0)
    def _():
        key_row = lax.broadcasted_iota(jnp.int32, (TOK, TOK), 0)
        query_row = lax.broadcasted_iota(jnp.int32, (TOK, TOK), 1)
        eye[...] = jnp.where(key_row == query_row, 1.0, 0.0).astype(jnp.bfloat16)
        vals[:, HEAD_SIZE:] = jnp.ones((count * TOK, HEAD_SIZE), jnp.bfloat16)
        me = ctx[0]
        my_span = span_map[me]
        x, z, c = me // 4, me // 2 % 2, me % 2
        for block, (dx, dz, dc) in enumerate(units):
            source = (x + 4 - dx) % 4 * 4 + (z + dz) % 2 * 2 + (c + dc) % 2
            ahead = (span_map[source] - my_span) * TOK + key_row - query_row
            keys[block * TOK : (block + 1) * TOK, HEAD_SIZE:] = jnp.where(
                ahead > 0, HIDDEN, 0.0
            ).astype(jnp.bfloat16)

    for block in range(count):
        rows = slice(block * TOK, (block + 1) * TOK)
        keys[rows, :HEAD_SIZE] = k_refs[block][...]
        vals[rows, :HEAD_SIZE] = v_refs[block][...]
    one_hot = eye[...]
    place = section[0] % RING
    for steps in range(RING):
        slab = (place + steps) % RING if last else steps
        tile = group * RING + slab
        q = q_ref[:, pl.ds(pl.multiple_of(slab * PAIR, PAIR), PAIR)]
        q = jnp.concatenate(
            [
                jnp.concatenate([q[:, :HEAD_SIZE], one_hot], axis=1),
                jnp.concatenate([q[:, HEAD_SIZE:], one_hot], axis=1),
            ],
            axis=0,
        )
        scores = lax.dot_general(
            q, keys[...], (((1,), (1,)), ((), ())), preferred_element_type=jnp.float32
        )
        peak = jnp.max(scores, axis=1, keepdims=True)
        if not first:
            before = peak_in[tile]
            peak = jnp.maximum(peak, before[:, :1])
        weights = jnp.exp2((scores - peak) * EXP2_SCALE).astype(jnp.bfloat16)
        mixed = jnp.dot(weights, vals[...], preferred_element_type=jnp.float32)
        if not first:
            mixed = mixed + sums_in[tile] * jnp.exp2((before[:, :1] - peak) * EXP2_SCALE)
        if last:
            result = (mixed[:, :HEAD_SIZE] / mixed[:, HEAD_SIZE:]).astype(jnp.bfloat16)
            o_refs[steps][:, :HEAD_SIZE] = result[:TOK]
            o_refs[steps][:, HEAD_SIZE:] = result[TOK:]
        else:
            sums_out[tile] = mixed
            peak_out[tile] = jnp.broadcast_to(peak, (2 * TOK, HEAD_SIZE))


def attention(span_map, ctx, section, queries, held, names, state, chunk):
    first, last = state is None, chunk is not None
    base, parts = (chunk * PART, PART) if last else (0, KEY_VALUE_HEADS)
    count = len(names)
    units = [held[name] for name in names]
    whole = pl.BlockSpec(memory_space=pltpu.VMEM)
    tiles = KEY_VALUE_HEADS * RING
    if last:
        out_specs = [pl.BlockSpec((TOK, PAIR), lambda g, *_: (0, g))] * RING
        out_shape = [jax.ShapeDtypeStruct((TOK, PART * PAIR), jnp.bfloat16)] * RING
    else:
        out_specs = [whole] * 2
        out_shape = [
            jax.ShapeDtypeStruct((tiles, 2 * TOK, PAIR), jnp.float32),
            jax.ShapeDtypeStruct((tiles, 2 * TOK, HEAD_SIZE), jnp.float32),
        ]
    return pl.pallas_call(
        functools.partial(attention_kernel, names, base, first, last),
        grid_spec=pltpu.PrefetchScalarGridSpec(
            num_scalar_prefetch=3,
            grid=(parts,),
            in_specs=[pl.BlockSpec((TOK, GROUP * HEAD_SIZE), lambda g, *_: (0, base + g))]
            + [pl.BlockSpec((TOK, HEAD_SIZE), lambda g, *_: (0, base + g))] * count
            + [pl.BlockSpec((TOK, HEAD_SIZE), lambda g, *_: (0, KEY_VALUE_HEADS + base + g))]
            * count
            + ([] if first else [whole] * 2),
            out_specs=out_specs,
            scratch_shapes=[
                pltpu.VMEM((count * TOK, PAIR), jnp.bfloat16),
                pltpu.VMEM((count * TOK, PAIR), jnp.bfloat16),
                pltpu.VMEM((TOK, TOK), jnp.bfloat16),
            ],
        ),
        out_shape=out_shape,
        input_output_aliases={}
        if first or last
        else {4 + 2 * count: 0, 5 + 2 * count: 1},
        compiler_params=pltpu.CompilerParams(vmem_limit_bytes=VMEM_LIMIT),
        cost_estimate=pl.CostEstimate(
            flops=parts * GROUP * TOK * count * TOK * PAIR * 2 * 2,
            bytes_accessed=parts * (count * TOK + GROUP * TOK) * PAIR * 2,
            transcendentals=parts * GROUP * TOK * count * TOK,
        ),
        name="attention",
    )(
        pinned(span_map),
        ctx,
        section,
        pinned(queries),
        *units,
        *units,
        *([] if first else state),
    )


def total_kernel(a, b, c, d, o_ref):
    f32 = jnp.float32
    o_ref[...] = (
        a[...].astype(f32) + b[...].astype(f32) + (c[...].astype(f32) + d[...].astype(f32))
    ).astype(jnp.bfloat16)


def row_total(slabs):
    return pl.pallas_call(
        total_kernel,
        in_specs=[pl.BlockSpec(memory_space=pltpu.VMEM)] * RING,
        out_specs=pl.BlockSpec(memory_space=pltpu.VMEM),
        out_shape=jax.ShapeDtypeStruct((TOK, PART * PAIR), jnp.bfloat16),
        compiler_params=pltpu.CompilerParams(vmem_limit_bytes=4 * 2**20),
        name="row_total",
    )(*slabs)


def prefix_kernel(chunk, section, residual_ref, *refs):
    slabs, below, outs = refs[:RING], refs[RING : 2 * RING - 1], refs[2 * RING - 1 : 3 * RING - 1]
    ordered, summed = refs[3 * RING - 1 :]
    place, row = section[0] % RING, section[0] // RING
    for steps in range(RING):
        ordered[(place + RING - steps) % RING] = slabs[steps][...]
    for part in range(PART):
        columns = slice(part * PAIR, (part + 1) * PAIR)
        first = (chunk * PART + part) * GROUP * HEAD_SIZE + place * PAIR
        state = residual_ref[:, pl.ds(pl.multiple_of(first, PAIR), PAIR)].astype(jnp.float32)
        for steps, rows in enumerate(below, 1):
            earlier = rows[:, columns].astype(jnp.float32)
            state = state + jnp.where(row >= steps, earlier, 0.0)
        for layer in range(RING):
            state = state + ordered[layer, :, columns].astype(jnp.float32)
            summed[layer, :, columns] = state.astype(jnp.bfloat16)
    for steps in range(RING):
        outs[steps][...] = summed[(place + steps) % RING]


def prefix(section, residual, slabs, below, chunk):
    slab = jax.ShapeDtypeStruct((TOK, PART * PAIR), jnp.bfloat16)
    whole = pl.BlockSpec(memory_space=pltpu.VMEM)
    return pl.pallas_call(
        functools.partial(prefix_kernel, chunk),
        in_specs=[pl.BlockSpec(memory_space=pltpu.SMEM)] + [whole] * (2 * RING),
        out_specs=[whole] * RING,
        out_shape=[slab] * RING,
        scratch_shapes=[
            pltpu.VMEM((RING, TOK, PART * PAIR), jnp.bfloat16),
            pltpu.VMEM((RING, TOK, PART * PAIR), jnp.bfloat16),
        ],
        compiler_params=pltpu.CompilerParams(vmem_limit_bytes=8 * 2**20),
        name="prefix",
    )(section, residual, *slabs, *below)


def assemble_kernel(section, *refs):
    slabs, o_ref = refs[:-1], refs[-1]
    place = section[0] % RING
    for chunk in range(CHUNKS):
        for steps in range(RING):
            column = (place + RING - steps) % RING * PAIR
            for part in range(PART):
                first = (chunk * PART + part) * GROUP * HEAD_SIZE + column
                o_ref[0, :, pl.ds(pl.multiple_of(first, PAIR), PAIR)] = slabs[
                    chunk * RING + steps
                ][:, part * PAIR : (part + 1) * PAIR]


def assemble(section, slabs):
    whole = pl.BlockSpec(memory_space=pltpu.VMEM)
    width = KEY_VALUE_HEADS * GROUP * HEAD_SIZE
    return pl.pallas_call(
        assemble_kernel,
        in_specs=[pl.BlockSpec(memory_space=pltpu.SMEM)] + [whole] * len(slabs),
        out_specs=whole,
        out_shape=jax.ShapeDtypeStruct((1, TOK, width), jnp.bfloat16),
        compiler_params=pltpu.CompilerParams(vmem_limit_bytes=8 * 2**20),
        name="assemble",
    )(section, *slabs)


def turn(slabs):
    return [slabs[0]] + [
        lax.ppermute(slabs[steps], "section", turn_pairs(steps)) for steps in range(1, RING)
    ]


def body(queries, keys, values, residual, span_map):
    ctx = lax.axis_index("ctx")[None]
    section = lax.axis_index("section")[None]
    held = gather(keys, values)
    attend = functools.partial(attention, span_map, ctx, section, queries[0], held)
    state = attend(EARLY, None, None)
    state = attend(MIDDLE, state, None)
    slabs = [turn(attend(LATE, state, chunk)) for chunk in range(CHUNKS)]
    finished, sums = [], None
    for chunk in range(CHUNKS):
        total = row_total(slabs[chunk])
        if sums is not None:
            total, *sums = lax.optimization_barrier((total, *sums))
            finished += turn(sums)
        below = [lax.ppermute(total, "section", climb_pairs(s)) for s in range(1, RING)]
        sums = prefix(section, residual, slabs[chunk], below, chunk)
    finished += turn(sums)
    return assemble(section, finished)


def solution(mesh):
    placed = (
        P("section", "ctx", None),
        P("section", "ctx", None),
        P("section", "ctx", None),
        P("ctx", None),
        P(),
    )
    return jax.shard_map(
        body, mesh=mesh, in_specs=placed, out_specs=P("section", "ctx", None), check_vma=False
    )
```

```python
import functools
import math

import jax
import jax.numpy as jnp
from jax import lax
from jax.experimental import pallas as pl
from jax.experimental.pallas import tpu as pltpu
from jax.sharding import PartitionSpec as P

KEY_VALUE_HEADS = 4
GROUP = 8
HEAD_SIZE = 128
TOK = 128
SPANS = 16
TRACE = SPANS * TOK
WIDTH = KEY_VALUE_HEADS * HEAD_SIZE
RING = 4
PAIR = 2 * HEAD_SIZE
EXP2_SCALE = math.log2(math.e) / math.sqrt(HEAD_SIZE)
HIDDEN = -1e30
VMEM_LIMIT = 24 * 2**20
CHUNKS = 2
PART = KEY_VALUE_HEADS // CHUNKS

SIDE = PART * HEAD_SIZE

NEAR = [(0, 0), (0, 1), (1, 0), (3, 0), (2, 0), (1, 1), (3, 1)]
WHOLE = 2 * len(NEAR)
UNITS = [(dx, dz, dc) for dc in range(2) for dx, dz in NEAR] + [(2, 1, 0), (2, 1, 1)]


def ctx_pairs(dx, dz, dc):
    pairs = []
    for i in range(SPANS):
        x, z, c = i // 4, i // 2 % 2, i % 2
        pairs.append((i, (x + dx) % 4 * 4 + (z ^ dz) * 2 + (c ^ dc)))
    return pairs


def ctx_move(unit, dx, dz, dc):
    return lax.ppermute(unit, "ctx", ctx_pairs(dx, dz, dc))


def turn_pairs(steps):
    return [(i, i // RING * RING + (i + steps) % RING) for i in range(RING * RING)]


def climb_pairs(steps):
    return [(i, (i + RING * steps) % (RING * RING)) for i in range(RING * RING)]


def pinned(x):
    return pltpu.with_memory_space_constraint(x, pltpu.HBM)


def join_kernel(k_ref, v_ref, o_ref, sems):
    copies = []
    for chunk in range(CHUNKS):
        for side, source in enumerate((k_ref, v_ref)):
            copies.append(
                pltpu.make_async_copy(
                    source.at[0, :, pl.ds(chunk * SIDE, SIDE)],
                    o_ref.at[:, pl.ds((2 * chunk + side) * SIDE, SIDE)],
                    sems.at[chunk, side],
                )
            )
    for copy in copies:
        copy.start()
    for copy in copies:
        copy.wait()


def join(keys, values):
    return pl.pallas_call(
        join_kernel,
        in_specs=[pl.BlockSpec(memory_space=pltpu.HBM)] * 2,
        out_specs=pl.BlockSpec(memory_space=pltpu.VMEM),
        out_shape=jax.ShapeDtypeStruct((TOK, 2 * WIDTH), jnp.bfloat16),
        scratch_shapes=[pltpu.SemaphoreType.DMA((CHUNKS, 2))],
        compiler_params=pltpu.CompilerParams(vmem_limit_bytes=2 * 2**20),
        name="join",
    )(pinned(keys), pinned(values))


def gather(keys, values):
    held = {(0, 0, 0): join(keys, values)}
    for dx, dz, source in (
        (0, 1, (0, 0, 0)),
        (1, 0, (0, 0, 0)),
        (3, 0, (0, 0, 0)),
        (0, 1, (1, 0, 0)),
        (1, 0, (1, 0, 0)),
        (3, 0, (0, 1, 0)),
    ):
        target = ((source[0] + dx) % 4, source[1] ^ dz, 0)
        held[target] = ctx_move(held[source], dx, dz, 0)
    farthest = [
        ctx_move(held[2, 0, 0][:, :WIDTH], 0, 1, 0),
        ctx_move(held[1, 1, 0][:, WIDTH:], 1, 0, 0),
    ]
    whole = [held[unit] for unit in UNITS[: len(NEAR)]]
    whole += [ctx_move(unit, 0, 0, 1) for unit in whole]
    halves = [[part, ctx_move(part, 0, 0, 1)] for part in farthest]
    return whole, halves


def attention_kernel(chunk, span_map, ctx, section, q_hbm, *refs):
    units, o_refs = refs[:SPANS], refs[SPANS : SPANS + RING]
    q_ref, keys, vals, sems = refs[SPANS + RING :]
    copies = []
    for part in range(PART):
        width = GROUP * HEAD_SIZE
        copies.append(
            pltpu.make_async_copy(
                q_hbm.at[:, pl.ds((chunk * PART + part) * width, width)],
                q_ref.at[part],
                sems.at[part],
            )
        )
        copies[-1].start()

    key_row = lax.broadcasted_iota(jnp.int32, (TOK, TOK), 0)
    query_row = lax.broadcasted_iota(jnp.int32, (TOK, TOK), 1)
    one_hot = jnp.where(key_row == query_row, 1.0, 0.0).astype(jnp.bfloat16)
    me = ctx[0]
    my_span = span_map[me]
    x, z, c = me // 4, me // 2 % 2, me % 2
    for block, (dx, dz, dc) in enumerate(UNITS):
        source = (x + 4 - dx) % 4 * 4 + (z + dz) % 2 * 2 + (c + dc) % 2
        ahead = (span_map[source] - my_span) * TOK + key_row - query_row
        mask = jnp.where(ahead > 0, HIDDEN, 0.0).astype(jnp.bfloat16)
        rows = slice(block * TOK, (block + 1) * TOK)
        start = chunk * 2 * SIDE if block < WHOLE else 0
        for part in range(PART):
            first = start + part * HEAD_SIZE
            keys[part, rows, :HEAD_SIZE] = units[block][:, first : first + HEAD_SIZE]
            keys[part, rows, HEAD_SIZE:] = mask
            first += SIDE
            vals[part, rows, :HEAD_SIZE] = units[block][:, first : first + HEAD_SIZE]
    for part in range(PART):
        vals[part, :, HEAD_SIZE:] = jnp.ones((TRACE, HEAD_SIZE), jnp.bfloat16)
    place = section[0] % RING

    def score(part, steps):
        first = pl.multiple_of((place + steps) % RING * PAIR, PAIR)
        q = q_ref[part, :, pl.ds(first, PAIR)]
        q = jnp.concatenate(
            [
                jnp.concatenate([q[:, :HEAD_SIZE], one_hot], axis=1),
                jnp.concatenate([q[:, HEAD_SIZE:], one_hot], axis=1),
            ],
            axis=0,
        )
        return lax.dot_general(
            q, keys[part], (((1,), (1,)), ((), ())), preferred_element_type=jnp.float32
        )

    def weigh(scores):
        peak = jnp.max(scores, axis=1, keepdims=True)
        return jnp.exp2((scores - peak) * EXP2_SCALE).astype(jnp.bfloat16)

    def mix(weights, part, steps):
        mixed = jnp.dot(weights, vals[part], preferred_element_type=jnp.float32)
        result = (mixed[:, :HEAD_SIZE] / mixed[:, HEAD_SIZE:]).astype(jnp.bfloat16)
        first = part * PAIR
        o_refs[steps][:, first : first + HEAD_SIZE] = result[:TOK]
        o_refs[steps][:, first + HEAD_SIZE : first + PAIR] = result[TOK:]

    tiles = [(part, steps) for part in range(PART) for steps in range(RING)]
    scores = weights = None
    for turn_index in range(len(tiles) + 2):
        if turn_index < len(tiles):
            if tiles[turn_index][1] == 0:
                copies[tiles[turn_index][0]].wait()
            upcoming = score(*tiles[turn_index])
        else:
            upcoming = None
        if weights is not None:
            mix(weights, *tiles[turn_index - 2])
        weights = None if scores is None else weigh(scores)
        scores = upcoming


def attention(span_map, ctx, section, queries, units, chunk):
    whole, halves = units
    units = whole + halves[chunk]
    smem = pl.BlockSpec(memory_space=pltpu.SMEM)
    vmem = pl.BlockSpec(memory_space=pltpu.VMEM)
    return pl.pallas_call(
        functools.partial(attention_kernel, chunk),
        in_specs=[smem, smem, smem, pl.BlockSpec(memory_space=pltpu.HBM)] + [vmem] * SPANS,
        out_specs=[vmem] * RING,
        out_shape=[jax.ShapeDtypeStruct((TOK, PART * PAIR), jnp.bfloat16)] * RING,
        scratch_shapes=[
            pltpu.VMEM((PART, TOK, GROUP * HEAD_SIZE), jnp.bfloat16),
            pltpu.VMEM((PART, TRACE, PAIR), jnp.bfloat16),
            pltpu.VMEM((PART, TRACE, PAIR), jnp.bfloat16),
            pltpu.SemaphoreType.DMA((PART,)),
        ],
        compiler_params=pltpu.CompilerParams(vmem_limit_bytes=VMEM_LIMIT),
        cost_estimate=pl.CostEstimate(
            flops=PART * GROUP * TOK * TRACE * PAIR * 2 * 2,
            bytes_accessed=PART * (TRACE * PAIR + GROUP * TOK * PAIR) * 2,
            transcendentals=PART * GROUP * TOK * TRACE,
        ),
        name="attention",
    )(pinned(span_map), ctx, section, pinned(queries), *units)


def total_kernel(a, b, c, d, o_ref):
    f32 = jnp.float32
    o_ref[...] = (
        a[...].astype(f32) + b[...].astype(f32) + (c[...].astype(f32) + d[...].astype(f32))
    ).astype(jnp.bfloat16)


def row_total(slabs):
    return pl.pallas_call(
        total_kernel,
        in_specs=[pl.BlockSpec(memory_space=pltpu.VMEM)] * RING,
        out_specs=pl.BlockSpec(memory_space=pltpu.VMEM),
        out_shape=jax.ShapeDtypeStruct((TOK, PART * PAIR), jnp.bfloat16),
        compiler_params=pltpu.CompilerParams(vmem_limit_bytes=4 * 2**20),
        name="row_total",
    )(*slabs)


def prefix_kernel(chunk, section, residual_ref, *refs):
    slabs, below, outs = refs[:RING], refs[RING : 2 * RING - 1], refs[2 * RING - 1 : 3 * RING - 1]
    ordered, summed = refs[3 * RING - 1 :]
    place, row = section[0] % RING, section[0] // RING
    for steps in range(RING):
        ordered[(place + RING - steps) % RING] = slabs[steps][...]
    for part in range(PART):
        columns = slice(part * PAIR, (part + 1) * PAIR)
        first = (chunk * PART + part) * GROUP * HEAD_SIZE + place * PAIR
        state = residual_ref[:, pl.ds(pl.multiple_of(first, PAIR), PAIR)].astype(jnp.float32)
        for steps, rows in enumerate(below, 1):
            earlier = rows[:, columns].astype(jnp.float32)
            state = state + jnp.where(row >= steps, earlier, 0.0)
        for layer in range(RING):
            state = state + ordered[layer, :, columns].astype(jnp.float32)
            summed[layer, :, columns] = state.astype(jnp.bfloat16)
    for steps in range(RING):
        outs[steps][...] = summed[(place + steps) % RING]


def prefix(section, residual, slabs, below, chunk):
    slab = jax.ShapeDtypeStruct((TOK, PART * PAIR), jnp.bfloat16)
    whole = pl.BlockSpec(memory_space=pltpu.VMEM)
    return pl.pallas_call(
        functools.partial(prefix_kernel, chunk),
        in_specs=[pl.BlockSpec(memory_space=pltpu.SMEM)] + [whole] * (2 * RING),
        out_specs=[whole] * RING,
        out_shape=[slab] * RING,
        scratch_shapes=[
            pltpu.VMEM((RING, TOK, PART * PAIR), jnp.bfloat16),
            pltpu.VMEM((RING, TOK, PART * PAIR), jnp.bfloat16),
        ],
        compiler_params=pltpu.CompilerParams(vmem_limit_bytes=8 * 2**20),
        name="prefix",
    )(section, residual, *slabs, *below)


def assemble_kernel(section, *refs):
    slabs, o_ref = refs[:-1], refs[-1]
    place = section[0] % RING
    for chunk in range(CHUNKS):
        for steps in range(RING):
            column = (place + RING - steps) % RING * PAIR
            for part in range(PART):
                first = (chunk * PART + part) * GROUP * HEAD_SIZE + column
                o_ref[0, :, pl.ds(pl.multiple_of(first, PAIR), PAIR)] = slabs[
                    chunk * RING + steps
                ][:, part * PAIR : (part + 1) * PAIR]


def assemble(section, slabs):
    whole = pl.BlockSpec(memory_space=pltpu.VMEM)
    width = KEY_VALUE_HEADS * GROUP * HEAD_SIZE
    return pl.pallas_call(
        assemble_kernel,
        in_specs=[pl.BlockSpec(memory_space=pltpu.SMEM)] + [whole] * len(slabs),
        out_specs=whole,
        out_shape=jax.ShapeDtypeStruct((1, TOK, width), jnp.bfloat16),
        compiler_params=pltpu.CompilerParams(vmem_limit_bytes=8 * 2**20),
        name="assemble",
    )(section, *slabs)


def turn(slabs):
    return [slabs[0]] + [
        lax.ppermute(slabs[steps], "section", turn_pairs(steps)) for steps in range(1, RING)
    ]


def body(queries, keys, values, residual, span_map):
    ctx = lax.axis_index("ctx")[None]
    section = lax.axis_index("section")[None]
    units = lax.optimization_barrier(gather(keys, values))
    raw = [attention(span_map, ctx, section, queries[0], units, c) for c in range(CHUNKS)]
    slabs = [turn(r) for r in raw]
    slabs[0], _ = lax.optimization_barrier((slabs[0], raw[1]))
    finished, sums = [], None
    for chunk in range(CHUNKS):
        if sums is not None:
            finished += turn(sums)
            slabs[chunk], finished[1], finished[3] = lax.optimization_barrier(
                (slabs[chunk], finished[1], finished[3])
            )
        total = row_total(slabs[chunk])
        below = [lax.ppermute(total, "section", climb_pairs(s)) for s in range(1, RING)]
        sums = prefix(section, residual, slabs[chunk], below, chunk)
    finished += turn(sums)
    return assemble(section, finished)


def solution(mesh):
    placed = (
        P("section", "ctx", None),
        P("section", "ctx", None),
        P("section", "ctx", None),
        P("ctx", None),
        P(),
    )
    return jax.shard_map(
        body, mesh=mesh, in_specs=placed, out_specs=P("section", "ctx", None), check_vma=False
    )
```

```python
import functools
import math

import jax
import jax.numpy as jnp
from jax import lax
from jax.experimental import pallas as pl
from jax.experimental.pallas import tpu as pltpu
from jax.sharding import PartitionSpec as P

KEY_VALUE_HEADS = 4
GROUP = 8
HEAD_SIZE = 128
TOK = 128
SPANS = 16
TRACE = SPANS * TOK
WIDTH = KEY_VALUE_HEADS * HEAD_SIZE
RING = 4
PAIR = 2 * HEAD_SIZE
EXP2_SCALE = math.log2(math.e) / math.sqrt(HEAD_SIZE)
HIDDEN = -1e30
VMEM_LIMIT = 24 * 2**20
CHUNKS = 2
PART = KEY_VALUE_HEADS // CHUNKS

SIDE = PART * HEAD_SIZE

UNITS = [(dx, dz, dc) for dc in range(2) for dz in range(2) for dx in range(4)]


def ctx_pairs(dx, dz, dc):
    pairs = []
    for i in range(SPANS):
        x, z, c = i // 4, i // 2 % 2, i % 2
        pairs.append((i, (x + dx) % 4 * 4 + (z ^ dz) * 2 + (c ^ dc)))
    return pairs


def ctx_move(unit, dx, dz, dc):
    return lax.ppermute(unit, "ctx", ctx_pairs(dx, dz, dc))


def turn_pairs(steps):
    return [(i, i // RING * RING + (i + steps) % RING) for i in range(RING * RING)]


def climb_pairs(steps):
    return [(i, (i + RING * steps) % (RING * RING)) for i in range(RING * RING)]


def pinned(x):
    return pltpu.with_memory_space_constraint(x, pltpu.HBM)


def join_kernel(k_ref, v_ref, o_ref, sems):
    copies = []
    for chunk in range(CHUNKS):
        for side, source in enumerate((k_ref, v_ref)):
            copies.append(
                pltpu.make_async_copy(
                    source.at[0, :, pl.ds(chunk * SIDE, SIDE)],
                    o_ref.at[:, pl.ds((2 * chunk + side) * SIDE, SIDE)],
                    sems.at[chunk, side],
                )
            )
    for copy in copies:
        copy.start()
    for copy in copies:
        copy.wait()


def join(keys, values):
    return pl.pallas_call(
        join_kernel,
        in_specs=[pl.BlockSpec(memory_space=pltpu.HBM)] * 2,
        out_specs=pl.BlockSpec(memory_space=pltpu.VMEM),
        out_shape=jax.ShapeDtypeStruct((TOK, 2 * WIDTH), jnp.bfloat16),
        scratch_shapes=[pltpu.SemaphoreType.DMA((CHUNKS, 2))],
        compiler_params=pltpu.CompilerParams(vmem_limit_bytes=2 * 2**20),
        name="join",
    )(pinned(keys), pinned(values))


def gather(keys, values):
    held = {(0, 0, 0): join(keys, values)}
    for dx, dz, source in (
        (0, 1, (0, 0, 0)),
        (1, 0, (0, 0, 0)),
        (3, 0, (0, 0, 0)),
        (0, 1, (1, 0, 0)),
        (1, 0, (1, 0, 0)),
        (3, 0, (0, 1, 0)),
        (0, 1, (2, 0, 0)),
    ):
        target = ((source[0] + dx) % 4, source[1] ^ dz, 0)
        held[target] = ctx_move(held[source], dx, dz, 0)
    for dz in range(2):
        for dx in range(4):
            held[dx, dz, 1] = ctx_move(held[dx, dz, 0], 0, 0, 1)
    return [held[unit] for unit in UNITS]


def attention_kernel(chunk, span_map, ctx, section, q_hbm, *refs):
    units, o_refs = refs[:SPANS], refs[SPANS : SPANS + RING]
    q_ref, keys, vals, sems = refs[SPANS + RING :]
    copies = []
    for part in range(PART):
        width = GROUP * HEAD_SIZE
        copies.append(
            pltpu.make_async_copy(
                q_hbm.at[:, pl.ds((chunk * PART + part) * width, width)],
                q_ref.at[part],
                sems.at[part],
            )
        )
        copies[-1].start()

    key_row = lax.broadcasted_iota(jnp.int32, (TOK, TOK), 0)
    query_row = lax.broadcasted_iota(jnp.int32, (TOK, TOK), 1)
    one_hot = jnp.where(key_row == query_row, 1.0, 0.0).astype(jnp.bfloat16)
    me = ctx[0]
    my_span = span_map[me]
    x, z, c = me // 4, me // 2 % 2, me % 2
    for block, (dx, dz, dc) in enumerate(UNITS):
        source = (x + 4 - dx) % 4 * 4 + (z + dz) % 2 * 2 + (c + dc) % 2
        ahead = (span_map[source] - my_span) * TOK + key_row - query_row
        mask = jnp.where(ahead > 0, HIDDEN, 0.0).astype(jnp.bfloat16)
        rows = slice(block * TOK, (block + 1) * TOK)
        for part in range(PART):
            first = chunk * 2 * SIDE + part * HEAD_SIZE
            keys[part, rows, :HEAD_SIZE] = units[block][:, first : first + HEAD_SIZE]
            keys[part, rows, HEAD_SIZE:] = mask
            first += SIDE
            vals[part, rows, :HEAD_SIZE] = units[block][:, first : first + HEAD_SIZE]
    for part in range(PART):
        vals[part, :, HEAD_SIZE:] = jnp.ones((TRACE, HEAD_SIZE), jnp.bfloat16)
    place = section[0] % RING

    def score(part, steps):
        first = pl.multiple_of((place + steps) % RING * PAIR, PAIR)
        q = q_ref[part, :, pl.ds(first, PAIR)]
        q = jnp.concatenate(
            [
                jnp.concatenate([q[:, :HEAD_SIZE], one_hot], axis=1),
                jnp.concatenate([q[:, HEAD_SIZE:], one_hot], axis=1),
            ],
            axis=0,
        )
        return lax.dot_general(
            q, keys[part], (((1,), (1,)), ((), ())), preferred_element_type=jnp.float32
        )

    def weigh(scores):
        peak = jnp.max(scores, axis=1, keepdims=True)
        return jnp.exp2((scores - peak) * EXP2_SCALE).astype(jnp.bfloat16)

    def mix(weights, part, steps):
        mixed = jnp.dot(weights, vals[part], preferred_element_type=jnp.float32)
        result = (mixed[:, :HEAD_SIZE] / mixed[:, HEAD_SIZE:]).astype(jnp.bfloat16)
        result = jnp.concatenate([result[:TOK], result[TOK:]], axis=1)
        o_refs[steps][:, pl.ds(pl.multiple_of(part * PAIR, PAIR), PAIR)] = result

    for copy in copies:
        copy.wait()

    @pl.loop(0, PART)
    def _(part):
        scores = weights = None
        for steps in range(RING + 2):
            upcoming = score(part, steps) if steps < RING else None
            if weights is not None:
                mix(weights, part, steps - 2)
            weights = None if scores is None else weigh(scores)
            scores = upcoming


def attention(span_map, ctx, section, queries, units, chunk):
    smem = pl.BlockSpec(memory_space=pltpu.SMEM)
    vmem = pl.BlockSpec(memory_space=pltpu.VMEM)
    return pl.pallas_call(
        functools.partial(attention_kernel, chunk),
        in_specs=[smem, smem, smem, pl.BlockSpec(memory_space=pltpu.HBM)] + [vmem] * SPANS,
        out_specs=[vmem] * RING,
        out_shape=[jax.ShapeDtypeStruct((TOK, PART * PAIR), jnp.bfloat16)] * RING,
        scratch_shapes=[
            pltpu.VMEM((PART, TOK, GROUP * HEAD_SIZE), jnp.bfloat16),
            pltpu.VMEM((PART, TRACE, PAIR), jnp.bfloat16),
            pltpu.VMEM((PART, TRACE, PAIR), jnp.bfloat16),
            pltpu.SemaphoreType.DMA((PART,)),
        ],
        compiler_params=pltpu.CompilerParams(vmem_limit_bytes=VMEM_LIMIT),
        cost_estimate=pl.CostEstimate(
            flops=PART * GROUP * TOK * TRACE * PAIR * 2 * 2,
            bytes_accessed=PART * (TRACE * PAIR + GROUP * TOK * PAIR) * 2,
            transcendentals=PART * GROUP * TOK * TRACE,
        ),
        name="attention",
    )(pinned(span_map), ctx, section, pinned(queries), *units)


def total_kernel(a, b, c, d, o_ref):
    f32 = jnp.float32
    o_ref[...] = (
        a[...].astype(f32) + b[...].astype(f32) + (c[...].astype(f32) + d[...].astype(f32))
    ).astype(jnp.bfloat16)


def row_total(slabs):
    return pl.pallas_call(
        total_kernel,
        in_specs=[pl.BlockSpec(memory_space=pltpu.VMEM)] * RING,
        out_specs=pl.BlockSpec(memory_space=pltpu.VMEM),
        out_shape=jax.ShapeDtypeStruct((TOK, PART * PAIR), jnp.bfloat16),
        compiler_params=pltpu.CompilerParams(vmem_limit_bytes=4 * 2**20),
        name="row_total",
    )(*slabs)


def prefix_kernel(chunk, section, residual_ref, *refs):
    slabs, below, outs = refs[:RING], refs[RING : 2 * RING - 1], refs[2 * RING - 1 : 3 * RING - 1]
    ordered, summed = refs[3 * RING - 1 :]
    place, row = section[0] % RING, section[0] // RING
    for steps in range(RING):
        ordered[(place + RING - steps) % RING] = slabs[steps][...]
    for part in range(PART):
        columns = slice(part * PAIR, (part + 1) * PAIR)
        first = (chunk * PART + part) * GROUP * HEAD_SIZE + place * PAIR
        state = residual_ref[:, pl.ds(pl.multiple_of(first, PAIR), PAIR)].astype(jnp.float32)
        for steps, rows in enumerate(below, 1):
            earlier = rows[:, columns].astype(jnp.float32)
            state = state + jnp.where(row >= steps, earlier, 0.0)
        for layer in range(RING):
            state = state + ordered[layer, :, columns].astype(jnp.float32)
            summed[layer, :, columns] = state.astype(jnp.bfloat16)
    for steps in range(RING):
        outs[steps][...] = summed[(place + steps) % RING]


def prefix(section, residual, slabs, below, chunk):
    slab = jax.ShapeDtypeStruct((TOK, PART * PAIR), jnp.bfloat16)
    whole = pl.BlockSpec(memory_space=pltpu.VMEM)
    return pl.pallas_call(
        functools.partial(prefix_kernel, chunk),
        in_specs=[pl.BlockSpec(memory_space=pltpu.SMEM)] + [whole] * (2 * RING),
        out_specs=[whole] * RING,
        out_shape=[slab] * RING,
        scratch_shapes=[
            pltpu.VMEM((RING, TOK, PART * PAIR), jnp.bfloat16),
            pltpu.VMEM((RING, TOK, PART * PAIR), jnp.bfloat16),
        ],
        compiler_params=pltpu.CompilerParams(vmem_limit_bytes=8 * 2**20),
        name="prefix",
    )(section, residual, *slabs, *below)


def assemble_kernel(section, *refs):
    slabs, o_ref = refs[:-1], refs[-1]
    place = section[0] % RING
    for chunk in range(CHUNKS):
        for steps in range(RING):
            column = (place + RING - steps) % RING * PAIR
            for part in range(PART):
                first = (chunk * PART + part) * GROUP * HEAD_SIZE + column
                o_ref[0, :, pl.ds(pl.multiple_of(first, PAIR), PAIR)] = slabs[
                    chunk * RING + steps
                ][:, part * PAIR : (part + 1) * PAIR]


def assemble(section, slabs):
    whole = pl.BlockSpec(memory_space=pltpu.VMEM)
    width = KEY_VALUE_HEADS * GROUP * HEAD_SIZE
    return pl.pallas_call(
        assemble_kernel,
        in_specs=[pl.BlockSpec(memory_space=pltpu.SMEM)] + [whole] * len(slabs),
        out_specs=whole,
        out_shape=jax.ShapeDtypeStruct((1, TOK, width), jnp.bfloat16),
        compiler_params=pltpu.CompilerParams(vmem_limit_bytes=8 * 2**20),
        name="assemble",
    )(section, *slabs)


def turn(slabs):
    return [slabs[0]] + [
        lax.ppermute(slabs[steps], "section", turn_pairs(steps)) for steps in range(1, RING)
    ]


def body(queries, keys, values, residual, span_map):
    ctx = lax.axis_index("ctx")[None]
    section = lax.axis_index("section")[None]
    units = gather(keys, values)
    slabs = [
        turn(attention(span_map, ctx, section, queries[0], units, chunk))
        for chunk in range(CHUNKS)
    ]
    finished, sums = [], None
    for chunk in range(CHUNKS):
        total = row_total(slabs[chunk])
        if sums is not None:
            total, *sums = lax.optimization_barrier((total, *sums))
            finished += turn(sums)
        below = [lax.ppermute(total, "section", climb_pairs(s)) for s in range(1, RING)]
        sums = prefix(section, residual, slabs[chunk], below, chunk)
    finished += turn(sums)
    return assemble(section, finished)


def solution(mesh):
    placed = (
        P("section", "ctx", None),
        P("section", "ctx", None),
        P("section", "ctx", None),
        P("ctx", None),
        P(),
    )
    return jax.shard_map(
        body, mesh=mesh, in_specs=placed, out_specs=P("section", "ctx", None), check_vma=False
    )
```

```python
import functools
import math

import jax
import jax.numpy as jnp
from jax import lax
from jax.experimental import pallas as pl
from jax.experimental.pallas import tpu as pltpu
from jax.sharding import PartitionSpec as P

KEY_VALUE_HEADS = 4
GROUP = 8
HEAD_SIZE = 128
TOK = 128
SPANS = 16
TRACE = SPANS * TOK
WIDTH = KEY_VALUE_HEADS * HEAD_SIZE
RING = 4
PAIR = 2 * HEAD_SIZE
EXP2_SCALE = math.log2(math.e) / math.sqrt(HEAD_SIZE)
HIDDEN = -1e30
VMEM_LIMIT = 20 * 2**20
CHUNKS = 2
PART = KEY_VALUE_HEADS // CHUNKS

SIDE = PART * HEAD_SIZE

UNITS = [(dx, dz, dc) for dc in range(2) for dz in range(2) for dx in range(4)]


def ctx_pairs(dx, dz, dc):
    pairs = []
    for i in range(SPANS):
        x, z, c = i // 4, i // 2 % 2, i % 2
        pairs.append((i, (x + dx) % 4 * 4 + (z ^ dz) * 2 + (c ^ dc)))
    return pairs


def ctx_move(unit, dx, dz, dc):
    return lax.ppermute(unit, "ctx", ctx_pairs(dx, dz, dc))


def turn_pairs(steps):
    return [(i, i // RING * RING + (i + steps) % RING) for i in range(RING * RING)]


def climb_pairs(steps):
    return [(i, (i + RING * steps) % (RING * RING)) for i in range(RING * RING)]


def pinned(x):
    return pltpu.with_memory_space_constraint(x, pltpu.HBM)


def join_kernel(k_ref, v_ref, o_ref, sems):
    copies = []
    for chunk in range(CHUNKS):
        for side, source in enumerate((k_ref, v_ref)):
            copies.append(
                pltpu.make_async_copy(
                    source.at[0, :, pl.ds(chunk * SIDE, SIDE)],
                    o_ref.at[:, pl.ds((2 * chunk + side) * SIDE, SIDE)],
                    sems.at[chunk, side],
                )
            )
    for copy in copies:
        copy.start()
    for copy in copies:
        copy.wait()


def join(keys, values):
    return pl.pallas_call(
        join_kernel,
        in_specs=[pl.BlockSpec(memory_space=pltpu.HBM)] * 2,
        out_specs=pl.BlockSpec(memory_space=pltpu.VMEM),
        out_shape=jax.ShapeDtypeStruct((TOK, 2 * WIDTH), jnp.bfloat16),
        scratch_shapes=[pltpu.SemaphoreType.DMA((CHUNKS, 2))],
        compiler_params=pltpu.CompilerParams(vmem_limit_bytes=2 * 2**20),
        name="join",
    )(pinned(keys), pinned(values))


def gather(keys, values):
    held = {(0, 0, 0): join(keys, values)}
    for dx, dz, source in (
        (0, 1, (0, 0, 0)),
        (1, 0, (0, 0, 0)),
        (3, 0, (0, 0, 0)),
        (0, 1, (1, 0, 0)),
        (1, 0, (1, 0, 0)),
        (3, 0, (0, 1, 0)),
        (0, 1, (2, 0, 0)),
    ):
        target = ((source[0] + dx) % 4, source[1] ^ dz, 0)
        held[target] = ctx_move(held[source], dx, dz, 0)
    for dz in range(2):
        for dx in range(4):
            held[dx, dz, 1] = ctx_move(held[dx, dz, 0], 0, 0, 1)
    return [held[unit] for unit in UNITS]


def attention_kernel(chunk, span_map, ctx, q_hbm, *refs):
    units, o_ref = refs[:SPANS], refs[SPANS]
    q_ref, keys, vals, sems = refs[SPANS + 1 :]
    copies = []
    for part in range(PART):
        width = GROUP * HEAD_SIZE
        copies.append(
            pltpu.make_async_copy(
                q_hbm.at[:, pl.ds((chunk * PART + part) * width, width)],
                q_ref.at[part],
                sems.at[part],
            )
        )
        copies[-1].start()

    key_row = lax.broadcasted_iota(jnp.int32, (TOK, TOK), 0)
    query_row = lax.broadcasted_iota(jnp.int32, (TOK, TOK), 1)
    one_hot = jnp.where(key_row == query_row, 1.0, 0.0).astype(jnp.bfloat16)
    me = ctx[0]
    my_span = span_map[me]
    x, z, c = me // 4, me // 2 % 2, me % 2
    for block, (dx, dz, dc) in enumerate(UNITS):
        source = (x + 4 - dx) % 4 * 4 + (z + dz) % 2 * 2 + (c + dc) % 2
        ahead = (span_map[source] - my_span) * TOK + key_row - query_row
        mask = jnp.where(ahead > 0, HIDDEN, 0.0).astype(jnp.bfloat16)
        rows = slice(block * TOK, (block + 1) * TOK)
        for part in range(PART):
            first = chunk * 2 * SIDE + part * HEAD_SIZE
            keys[part, rows, :HEAD_SIZE] = units[block][:, first : first + HEAD_SIZE]
            keys[part, rows, HEAD_SIZE:] = mask
            first += SIDE
            vals[part, rows, :HEAD_SIZE] = units[block][:, first : first + HEAD_SIZE]
    for part in range(PART):
        vals[part, :, HEAD_SIZE:] = jnp.ones((TRACE, HEAD_SIZE), jnp.bfloat16)

    def score(part, owner):
        q = q_ref[part, :, owner * PAIR : (owner + 1) * PAIR]
        q = jnp.concatenate(
            [
                jnp.concatenate([q[:, :HEAD_SIZE], one_hot], axis=1),
                jnp.concatenate([q[:, HEAD_SIZE:], one_hot], axis=1),
            ],
            axis=0,
        )
        return lax.dot_general(
            q, keys[part], (((1,), (1,)), ((), ())), preferred_element_type=jnp.float32
        )

    def weigh(scores):
        peak = jnp.max(scores, axis=1, keepdims=True)
        return jnp.exp2((scores - peak) * EXP2_SCALE).astype(jnp.bfloat16)

    def mix(weights, part, owner):
        mixed = jnp.dot(weights, vals[part], preferred_element_type=jnp.float32)
        result = (mixed[:, :HEAD_SIZE] / mixed[:, HEAD_SIZE:]).astype(jnp.bfloat16)
        result = jnp.concatenate([result[:TOK], result[TOK:]], axis=1)
        o_ref[owner, :, pl.ds(pl.multiple_of(part * PAIR, PAIR), PAIR)] = result

    for copy in copies:
        copy.wait()

    @pl.loop(0, PART)
    def _(part):
        scores = weights = None
        for owner in range(RING + 2):
            upcoming = score(part, owner) if owner < RING else None
            if weights is not None:
                mix(weights, part, owner - 2)
            weights = None if scores is None else weigh(scores)
            scores = upcoming


def attention(span_map, ctx, queries, units, chunk):
    smem = pl.BlockSpec(memory_space=pltpu.SMEM)
    vmem = pl.BlockSpec(memory_space=pltpu.VMEM)
    return pl.pallas_call(
        functools.partial(attention_kernel, chunk),
        in_specs=[smem, smem, pl.BlockSpec(memory_space=pltpu.HBM)] + [vmem] * SPANS,
        out_specs=vmem,
        out_shape=jax.ShapeDtypeStruct((RING, TOK, PART * PAIR), jnp.bfloat16),
        scratch_shapes=[
            pltpu.VMEM((PART, TOK, GROUP * HEAD_SIZE), jnp.bfloat16),
            pltpu.VMEM((PART, TRACE, PAIR), jnp.bfloat16),
            pltpu.VMEM((PART, TRACE, PAIR), jnp.bfloat16),
            pltpu.SemaphoreType.DMA((PART,)),
        ],
        compiler_params=pltpu.CompilerParams(vmem_limit_bytes=VMEM_LIMIT),
        cost_estimate=pl.CostEstimate(
            flops=PART * GROUP * TOK * TRACE * PAIR * 2 * 2,
            bytes_accessed=PART * (TRACE * PAIR + GROUP * TOK * PAIR) * 2,
            transcendentals=PART * GROUP * TOK * TRACE,
        ),
        name="attention",
    )(pinned(span_map), ctx, pinned(queries), *units)


def total_kernel(x_ref, o_ref):
    layers = [x_ref[layer].astype(jnp.float32) for layer in range(RING)]
    o_ref[...] = ((layers[0] + layers[1]) + (layers[2] + layers[3])).astype(jnp.bfloat16)


def row_total(layers):
    return pl.pallas_call(
        total_kernel,
        in_specs=[pl.BlockSpec(memory_space=pltpu.VMEM)],
        out_specs=pl.BlockSpec(memory_space=pltpu.VMEM),
        out_shape=jax.ShapeDtypeStruct((TOK, PART * PAIR), jnp.bfloat16),
        compiler_params=pltpu.CompilerParams(vmem_limit_bytes=4 * 2**20),
        name="row_total",
    )(layers)


def prefix_kernel(chunk, section, residual_ref, layers, *refs):
    below, outs, summed = refs[: RING - 1], refs[RING - 1 : -1], refs[-1]
    if len(outs) == 1:
        summed = outs[0]
    place, row = section[0] % RING, section[0] // RING
    for part in range(PART):
        columns = slice(part * PAIR, (part + 1) * PAIR)
        first = (chunk * PART + part) * GROUP * HEAD_SIZE + place * PAIR
        state = residual_ref[:, pl.ds(pl.multiple_of(first, PAIR), PAIR)].astype(jnp.float32)
        for steps, rows in enumerate(below, 1):
            earlier = rows[:, columns].astype(jnp.float32)
            state = state + jnp.where(row >= steps, earlier, 0.0)
        for layer in range(RING):
            state = state + layers[layer, :, columns].astype(jnp.float32)
            summed[layer, :, columns] = state.astype(jnp.bfloat16)
    if len(outs) > 1:
        for steps in range(RING):
            outs[steps][...] = summed[(place + steps) % RING]


def prefix(section, residual, layers, below, chunk, joint):
    shape = (TOK, PART * PAIR)
    whole = pl.BlockSpec(memory_space=pltpu.VMEM)
    outs = [(RING, *shape)] if joint else [shape] * RING
    return pl.pallas_call(
        functools.partial(prefix_kernel, chunk),
        in_specs=[pl.BlockSpec(memory_space=pltpu.SMEM)] + [whole] * (1 + RING),
        out_specs=[whole] * len(outs),
        out_shape=[jax.ShapeDtypeStruct(out, jnp.bfloat16) for out in outs],
        scratch_shapes=[pltpu.VMEM((RING, *shape), jnp.bfloat16)],
        compiler_params=pltpu.CompilerParams(vmem_limit_bytes=8 * 2**20),
        name="prefix",
    )(section, residual, layers, *below)


def assemble_kernel(joint, section, *refs):
    o_ref, refs = refs[-1], list(refs[:-1])
    place = section[0] % RING
    for chunk in range(CHUNKS):
        for steps in range(RING):
            if joint[chunk]:
                slab, owner = refs[0].at[steps], steps
            else:
                slab, owner = refs.pop(0), (place + RING - steps) % RING
            for part in range(PART):
                first = (chunk * PART + part) * GROUP * HEAD_SIZE + owner * PAIR
                if not joint[chunk]:
                    first = pl.multiple_of(first, PAIR)
                o_ref[0, :, pl.ds(first, PAIR)] = slab[:, part * PAIR : (part + 1) * PAIR]
        if joint[chunk]:
            refs.pop(0)


def assemble(section, slabs, joint):
    whole = pl.BlockSpec(memory_space=pltpu.VMEM)
    width = KEY_VALUE_HEADS * GROUP * HEAD_SIZE
    return pl.pallas_call(
        functools.partial(assemble_kernel, joint),
        in_specs=[pl.BlockSpec(memory_space=pltpu.SMEM)] + [whole] * len(slabs),
        out_specs=whole,
        out_shape=jax.ShapeDtypeStruct((1, TOK, width), jnp.bfloat16),
        compiler_params=pltpu.CompilerParams(vmem_limit_bytes=8 * 2**20),
        name="assemble",
    )(section, *slabs)


def turn(slabs):
    return [slabs[0]] + [
        lax.ppermute(slabs[steps], "section", turn_pairs(steps)) for steps in range(1, RING)
    ]


def swap(slabs):
    rows = [[y * RING + z for z in range(RING)] for y in range(RING)]
    return lax.all_to_all(slabs, "section", 0, 0, axis_index_groups=rows, tiled=True)


JOINT = (True, False)


def body(queries, keys, values, residual, span_map):
    ctx = lax.axis_index("ctx")[None]
    section = lax.axis_index("section")[None]
    units = gather(keys, values)
    layers = [swap(attention(span_map, ctx, queries[0], units, c)) for c in range(CHUNKS)]
    finished, sums = [], None
    for chunk in range(CHUNKS):
        total = row_total(layers[chunk])
        if sums is not None:
            total, *sums = lax.optimization_barrier((total, *sums))
            finished += [swap(sums[0])] if JOINT[0] else turn(sums)
        below = [lax.ppermute(total, "section", climb_pairs(s)) for s in range(1, RING)]
        sums = prefix(section, residual, layers[chunk], below, chunk, JOINT[chunk])
    finished += [swap(sums[0])] if JOINT[1] else turn(sums)
    return assemble(section, finished, JOINT)


def solution(mesh):
    placed = (
        P("section", "ctx", None),
        P("section", "ctx", None),
        P("section", "ctx", None),
        P("ctx", None),
        P(),
    )
    return jax.shard_map(
        body, mesh=mesh, in_specs=placed, out_specs=P("section", "ctx", None), check_vma=False
    )
```

```python
import functools
import math

import jax
import jax.numpy as jnp
from jax import lax
from jax.experimental import pallas as pl
from jax.experimental.pallas import tpu as pltpu
from jax.sharding import PartitionSpec as P

KEY_VALUE_HEADS = 4
GROUP = 8
HEAD_SIZE = 128
TOK = 128
SPANS = 16
TRACE = SPANS * TOK
WIDTH = KEY_VALUE_HEADS * HEAD_SIZE
RING = 4
PAIR = 2 * HEAD_SIZE
EXP2_SCALE = math.log2(math.e) / math.sqrt(HEAD_SIZE)
HIDDEN = -1e30
VMEM_LIMIT = 24 * 2**20
CHUNKS = 2
PART = KEY_VALUE_HEADS // CHUNKS

SIDE = PART * HEAD_SIZE

NEAR = [(0, 0), (0, 1), (1, 0), (3, 0), (2, 0), (3, 1), (1, 1)]
WHOLE = 2 * len(NEAR)
UNITS = [(dx, dz, dc) for dc in range(2) for dx, dz in NEAR] + [(2, 1, 0), (2, 1, 1)]


def ctx_pairs(dx, dz, dc):
    pairs = []
    for i in range(SPANS):
        x, z, c = i // 4, i // 2 % 2, i % 2
        pairs.append((i, (x + dx) % 4 * 4 + (z ^ dz) * 2 + (c ^ dc)))
    return pairs


def ctx_move(unit, dx, dz, dc):
    return lax.ppermute(unit, "ctx", ctx_pairs(dx, dz, dc))


def turn_pairs(steps):
    return [(i, i // RING * RING + (i + steps) % RING) for i in range(RING * RING)]


def climb_pairs(steps):
    return [(i, (i + RING * steps) % (RING * RING)) for i in range(RING * RING)]


def pinned(x):
    return pltpu.with_memory_space_constraint(x, pltpu.HBM)


def join_kernel(k_ref, v_ref, o_ref, sems):
    copies = []
    for chunk in range(CHUNKS):
        for side, source in enumerate((k_ref, v_ref)):
            copies.append(
                pltpu.make_async_copy(
                    source.at[0, :, pl.ds(chunk * SIDE, SIDE)],
                    o_ref.at[:, pl.ds((2 * chunk + side) * SIDE, SIDE)],
                    sems.at[chunk, side],
                )
            )
    for copy in copies:
        copy.start()
    for copy in copies:
        copy.wait()


def join(keys, values):
    return pl.pallas_call(
        join_kernel,
        in_specs=[pl.BlockSpec(memory_space=pltpu.HBM)] * 2,
        out_specs=pl.BlockSpec(memory_space=pltpu.VMEM),
        out_shape=jax.ShapeDtypeStruct((TOK, 2 * WIDTH), jnp.bfloat16),
        scratch_shapes=[pltpu.SemaphoreType.DMA((CHUNKS, 2))],
        compiler_params=pltpu.CompilerParams(vmem_limit_bytes=2 * 2**20),
        name="join",
    )(pinned(keys), pinned(values))


def pack_kernel(*refs):
    for place, ref in enumerate(refs[:-1]):
        refs[-1][place] = ref[...]


def pack(units):
    vmem = pl.BlockSpec(memory_space=pltpu.VMEM)
    return pl.pallas_call(
        pack_kernel,
        in_specs=[vmem] * len(units),
        out_specs=vmem,
        out_shape=jax.ShapeDtypeStruct((len(units), *units[0].shape), jnp.bfloat16),
        compiler_params=pltpu.CompilerParams(vmem_limit_bytes=4 * 2**20),
        name="pack",
    )(*units)


def gather(keys, values):
    own = join(keys, values)
    back1 = ctx_move(own, 1, 0, 0)
    other = ctx_move(own, 0, 1, 0)
    back3 = ctx_move(own, 3, 0, 0)
    back2 = ctx_move(back1, 1, 0, 0)
    other1 = ctx_move(back1, 0, 1, 0)
    other3 = ctx_move(other, 3, 0, 0)
    farthest = [
        ctx_move(back2[:, :WIDTH], 0, 1, 0),
        ctx_move(other1[:, WIDTH:], 1, 0, 0),
    ]
    shared = [own, pack([other, back1, back3]), pack([back2, other3, other1])]
    shared += [ctx_move(x, 0, 0, 1) for x in shared]
    halves = [[part, ctx_move(part, 0, 0, 1)] for part in farthest]
    return shared, halves


def attention_kernel(chunk, span_map, ctx, section, q_hbm, *refs):
    held, o_refs = refs[:8], refs[8 : 8 + RING]
    q_ref, keys, vals, sems = refs[8 + RING :]
    units = []
    for side in range(2):
        own, near, later = held[3 * side : 3 * side + 3]
        units += [own] + [x.at[i] for x in (near, later) for i in range(3)]
    units += held[6:]
    copies = []
    for part in range(PART):
        width = GROUP * HEAD_SIZE
        copies.append(
            pltpu.make_async_copy(
                q_hbm.at[:, pl.ds((chunk * PART + part) * width, width)],
                q_ref.at[part],
                sems.at[part],
            )
        )
        copies[-1].start()

    key_row = lax.broadcasted_iota(jnp.int32, (TOK, TOK), 0)
    query_row = lax.broadcasted_iota(jnp.int32, (TOK, TOK), 1)
    one_hot = jnp.where(key_row == query_row, 1.0, 0.0).astype(jnp.bfloat16)
    me = ctx[0]
    my_span = span_map[me]
    x, z, c = me // 4, me // 2 % 2, me % 2
    for block, (dx, dz, dc) in enumerate(UNITS):
        source = (x + 4 - dx) % 4 * 4 + (z + dz) % 2 * 2 + (c + dc) % 2
        ahead = (span_map[source] - my_span) * TOK + key_row - query_row
        mask = jnp.where(ahead > 0, HIDDEN, 0.0).astype(jnp.bfloat16)
        rows = slice(block * TOK, (block + 1) * TOK)
        for part in range(PART):
            first = part * HEAD_SIZE + (chunk * 2 * SIDE if block < WHOLE else 0)
            keys[part, rows, :HEAD_SIZE] = units[block][:, first : first + HEAD_SIZE]
            keys[part, rows, HEAD_SIZE:] = mask
            first += SIDE
            vals[part, rows, :HEAD_SIZE] = units[block][:, first : first + HEAD_SIZE]
    for part in range(PART):
        vals[part, :, HEAD_SIZE:] = jnp.ones((TRACE, HEAD_SIZE), jnp.bfloat16)
    place = section[0] % RING

    def score(part, steps):
        first = pl.multiple_of((place + steps) % RING * PAIR, PAIR)
        q = q_ref[part, :, pl.ds(first, PAIR)]
        q = jnp.concatenate(
            [
                jnp.concatenate([q[:, :HEAD_SIZE], one_hot], axis=1),
                jnp.concatenate([q[:, HEAD_SIZE:], one_hot], axis=1),
            ],
            axis=0,
        )
        return lax.dot_general(
            q, keys[part], (((1,), (1,)), ((), ())), preferred_element_type=jnp.float32
        )

    def weigh(scores):
        peak = jnp.max(scores, axis=1, keepdims=True)
        return jnp.exp2((scores - peak) * EXP2_SCALE).astype(jnp.bfloat16)

    def mix(weights, part, steps):
        mixed = jnp.dot(weights, vals[part], preferred_element_type=jnp.float32)
        result = (mixed[:, :HEAD_SIZE] / mixed[:, HEAD_SIZE:]).astype(jnp.bfloat16)
        result = jnp.concatenate([result[:TOK], result[TOK:]], axis=1)
        o_refs[steps][:, pl.ds(pl.multiple_of(part * PAIR, PAIR), PAIR)] = result

    for copy in copies:
        copy.wait()

    @pl.loop(0, PART)
    def _(part):
        scores = weights = None
        for steps in range(RING + 2):
            upcoming = score(part, steps) if steps < RING else None
            if weights is not None:
                mix(weights, part, steps - 2)
            weights = None if scores is None else weigh(scores)
            scores = upcoming


def attention(span_map, ctx, section, queries, units, chunk):
    shared, halves = units
    units = [*shared, *halves[chunk]]
    smem = pl.BlockSpec(memory_space=pltpu.SMEM)
    vmem = pl.BlockSpec(memory_space=pltpu.VMEM)
    return pl.pallas_call(
        functools.partial(attention_kernel, chunk),
        in_specs=[smem, smem, smem, pl.BlockSpec(memory_space=pltpu.HBM)] + [vmem] * 8,
        out_specs=[vmem] * RING,
        out_shape=[jax.ShapeDtypeStruct((TOK, PART * PAIR), jnp.bfloat16)] * RING,
        scratch_shapes=[
            pltpu.VMEM((PART, TOK, GROUP * HEAD_SIZE), jnp.bfloat16),
            pltpu.VMEM((PART, TRACE, PAIR), jnp.bfloat16),
            pltpu.VMEM((PART, TRACE, PAIR), jnp.bfloat16),
            pltpu.SemaphoreType.DMA((PART,)),
        ],
        compiler_params=pltpu.CompilerParams(vmem_limit_bytes=VMEM_LIMIT),
        cost_estimate=pl.CostEstimate(
            flops=PART * GROUP * TOK * TRACE * PAIR * 2 * 2,
            bytes_accessed=PART * (TRACE * PAIR + GROUP * TOK * PAIR) * 2,
            transcendentals=PART * GROUP * TOK * TRACE,
        ),
        name="attention",
    )(pinned(span_map), ctx, section, pinned(queries), *units)


def total_kernel(a, b, c, d, o_ref):
    f32 = jnp.float32
    o_ref[...] = (
        a[...].astype(f32) + b[...].astype(f32) + (c[...].astype(f32) + d[...].astype(f32))
    ).astype(jnp.bfloat16)


def row_total(slabs):
    return pl.pallas_call(
        total_kernel,
        in_specs=[pl.BlockSpec(memory_space=pltpu.VMEM)] * RING,
        out_specs=pl.BlockSpec(memory_space=pltpu.VMEM),
        out_shape=jax.ShapeDtypeStruct((TOK, PART * PAIR), jnp.bfloat16),
        compiler_params=pltpu.CompilerParams(vmem_limit_bytes=4 * 2**20),
        name="row_total",
    )(*slabs)


def prefix_kernel(chunk, section, residual_ref, *refs):
    slabs, below, outs = refs[:RING], refs[RING : 2 * RING - 1], refs[2 * RING - 1 : 3 * RING - 1]
    ordered, summed = refs[3 * RING - 1 :]
    place, row = section[0] % RING, section[0] // RING
    for steps in range(RING):
        ordered[(place + RING - steps) % RING] = slabs[steps][...]
    for part in range(PART):
        columns = slice(part * PAIR, (part + 1) * PAIR)
        first = (chunk * PART + part) * GROUP * HEAD_SIZE + place * PAIR
        state = residual_ref[:, pl.ds(pl.multiple_of(first, PAIR), PAIR)].astype(jnp.float32)
        for steps, rows in enumerate(below, 1):
            earlier = rows[:, columns].astype(jnp.float32)
            state = state + jnp.where(row >= steps, earlier, 0.0)
        for layer in range(RING):
            state = state + ordered[layer, :, columns].astype(jnp.float32)
            summed[layer, :, columns] = state.astype(jnp.bfloat16)
    for steps in range(RING):
        outs[steps][...] = summed[(place + steps) % RING]


def prefix(section, residual, slabs, below, chunk):
    slab = jax.ShapeDtypeStruct((TOK, PART * PAIR), jnp.bfloat16)
    whole = pl.BlockSpec(memory_space=pltpu.VMEM)
    return pl.pallas_call(
        functools.partial(prefix_kernel, chunk),
        in_specs=[pl.BlockSpec(memory_space=pltpu.SMEM)] + [whole] * (2 * RING),
        out_specs=[whole] * RING,
        out_shape=[slab] * RING,
        scratch_shapes=[
            pltpu.VMEM((RING, TOK, PART * PAIR), jnp.bfloat16),
            pltpu.VMEM((RING, TOK, PART * PAIR), jnp.bfloat16),
        ],
        compiler_params=pltpu.CompilerParams(vmem_limit_bytes=8 * 2**20),
        name="prefix",
    )(section, residual, *slabs, *below)


def assemble_kernel(section, *refs):
    slabs, o_ref = refs[:-1], refs[-1]
    place = section[0] % RING
    for chunk in range(CHUNKS):
        for steps in range(RING):
            column = (place + RING - steps) % RING * PAIR
            for part in range(PART):
                first = (chunk * PART + part) * GROUP * HEAD_SIZE + column
                o_ref[0, :, pl.ds(pl.multiple_of(first, PAIR), PAIR)] = slabs[
                    chunk * RING + steps
                ][:, part * PAIR : (part + 1) * PAIR]


def assemble(section, slabs):
    whole = pl.BlockSpec(memory_space=pltpu.VMEM)
    width = KEY_VALUE_HEADS * GROUP * HEAD_SIZE
    return pl.pallas_call(
        assemble_kernel,
        in_specs=[pl.BlockSpec(memory_space=pltpu.SMEM)] + [whole] * len(slabs),
        out_specs=whole,
        out_shape=jax.ShapeDtypeStruct((1, TOK, width), jnp.bfloat16),
        compiler_params=pltpu.CompilerParams(vmem_limit_bytes=8 * 2**20),
        name="assemble",
    )(section, *slabs)


def turn(slabs):
    return [slabs[0]] + [
        lax.ppermute(slabs[steps], "section", turn_pairs(steps)) for steps in range(1, RING)
    ]


def body(queries, keys, values, residual, span_map):
    ctx = lax.axis_index("ctx")[None]
    section = lax.axis_index("section")[None]
    units = lax.optimization_barrier(gather(keys, values))
    slabs = [
        turn(attention(span_map, ctx, section, queries[0], units, chunk))
        for chunk in range(CHUNKS)
    ]
    finished, sums = [], None
    for chunk in range(CHUNKS):
        total = row_total(slabs[chunk])
        if sums is not None:
            total, *sums = lax.optimization_barrier((total, *sums))
            finished += turn(sums)
        below = [lax.ppermute(total, "section", climb_pairs(s)) for s in range(1, RING)]
        sums = prefix(section, residual, slabs[chunk], below, chunk)
    finished += turn(sums)
    return assemble(section, finished)


def solution(mesh):
    placed = (
        P("section", "ctx", None),
        P("section", "ctx", None),
        P("section", "ctx", None),
        P("ctx", None),
        P(),
    )
    return jax.shard_map(
        body, mesh=mesh, in_specs=placed, out_specs=P("section", "ctx", None), check_vma=False
    )
```

```python
import functools
import math

import jax
import jax.numpy as jnp
from jax import lax
from jax.experimental import pallas as pl
from jax.experimental.pallas import tpu as pltpu
from jax.sharding import PartitionSpec as P

KEY_VALUE_HEADS = 4
GROUP = 8
HEAD_SIZE = 128
TOK = 128
SPANS = 16
TRACE = SPANS * TOK
WIDTH = KEY_VALUE_HEADS * HEAD_SIZE
RING = 4
PAIR = 2 * HEAD_SIZE
EXP2_SCALE = math.log2(math.e) / math.sqrt(HEAD_SIZE)
HIDDEN = -1e30
VMEM_LIMIT = 24 * 2**20
CHUNKS = 2
PARTS = (3, 1)
BASES = (0, 3)

UNITS = [(dx, dz, dc) for dc in range(2) for dz in range(2) for dx in range(4)]


def ctx_pairs(dx, dz, dc):
    pairs = []
    for i in range(SPANS):
        x, z, c = i // 4, i // 2 % 2, i % 2
        pairs.append((i, (x + dx) % 4 * 4 + (z ^ dz) * 2 + (c ^ dc)))
    return pairs


def ctx_move(unit, dx, dz, dc):
    return lax.ppermute(unit, "ctx", ctx_pairs(dx, dz, dc))


def turn_pairs(steps):
    return [(i, i // RING * RING + (i + steps) % RING) for i in range(RING * RING)]


def climb_pairs(steps):
    return [(i, (i + RING * steps) % (RING * RING)) for i in range(RING * RING)]


def pinned(x):
    return pltpu.with_memory_space_constraint(x, pltpu.HBM)


def join_kernel(k_ref, v_ref, o_ref, sems):
    copies = []
    for chunk in range(CHUNKS):
        base, width = BASES[chunk] * HEAD_SIZE, PARTS[chunk] * HEAD_SIZE
        for side, source in enumerate((k_ref, v_ref)):
            copies.append(
                pltpu.make_async_copy(
                    source.at[0, :, pl.ds(base, width)],
                    o_ref.at[:, pl.ds(2 * base + side * width, width)],
                    sems.at[chunk, side],
                )
            )
    for copy in copies:
        copy.start()
    for copy in copies:
        copy.wait()


def join(keys, values):
    return pl.pallas_call(
        join_kernel,
        in_specs=[pl.BlockSpec(memory_space=pltpu.HBM)] * 2,
        out_specs=pl.BlockSpec(memory_space=pltpu.VMEM),
        out_shape=jax.ShapeDtypeStruct((TOK, 2 * WIDTH), jnp.bfloat16),
        scratch_shapes=[pltpu.SemaphoreType.DMA((CHUNKS, 2))],
        compiler_params=pltpu.CompilerParams(vmem_limit_bytes=2 * 2**20),
        name="join",
    )(pinned(keys), pinned(values))


def gather(keys, values):
    held = {(0, 0, 0): join(keys, values)}
    for dx, dz, source in (
        (0, 1, (0, 0, 0)),
        (1, 0, (0, 0, 0)),
        (3, 0, (0, 0, 0)),
        (0, 1, (1, 0, 0)),
        (1, 0, (1, 0, 0)),
        (3, 0, (0, 1, 0)),
        (0, 1, (2, 0, 0)),
    ):
        target = ((source[0] + dx) % 4, source[1] ^ dz, 0)
        held[target] = ctx_move(held[source], dx, dz, 0)
    for dz in range(2):
        for dx in range(4):
            held[dx, dz, 1] = ctx_move(held[dx, dz, 0], 0, 0, 1)
    return [held[unit] for unit in UNITS]


def attention_kernel(chunk, span_map, ctx, section, q_hbm, *refs):
    units, o_refs = refs[:SPANS], refs[SPANS : SPANS + RING]
    q_ref, keys, vals, sems = refs[SPANS + RING :]
    base, parts = BASES[chunk], PARTS[chunk]
    copies = []
    for part in range(parts):
        width = GROUP * HEAD_SIZE
        copies.append(
            pltpu.make_async_copy(
                q_hbm.at[:, pl.ds((base + part) * width, width)],
                q_ref.at[part],
                sems.at[part],
            )
        )
        copies[-1].start()

    key_row = lax.broadcasted_iota(jnp.int32, (TOK, TOK), 0)
    query_row = lax.broadcasted_iota(jnp.int32, (TOK, TOK), 1)
    one_hot = jnp.where(key_row == query_row, 1.0, 0.0).astype(jnp.bfloat16)
    me = ctx[0]
    my_span = span_map[me]
    x, z, c = me // 4, me // 2 % 2, me % 2
    for block, (dx, dz, dc) in enumerate(UNITS):
        source = (x + 4 - dx) % 4 * 4 + (z + dz) % 2 * 2 + (c + dc) % 2
        ahead = (span_map[source] - my_span) * TOK + key_row - query_row
        mask = jnp.where(ahead > 0, HIDDEN, 0.0).astype(jnp.bfloat16)
        rows = slice(block * TOK, (block + 1) * TOK)
        for part in range(parts):
            first = (2 * base + part) * HEAD_SIZE
            keys[part, rows, :HEAD_SIZE] = units[block][:, first : first + HEAD_SIZE]
            keys[part, rows, HEAD_SIZE:] = mask
            first += parts * HEAD_SIZE
            vals[part, rows, :HEAD_SIZE] = units[block][:, first : first + HEAD_SIZE]
    for part in range(parts):
        vals[part, :, HEAD_SIZE:] = jnp.ones((TRACE, HEAD_SIZE), jnp.bfloat16)
    place = section[0] % RING

    def score(part, steps):
        first = pl.multiple_of((place + steps) % RING * PAIR, PAIR)
        q = q_ref[part, :, pl.ds(first, PAIR)]
        q = jnp.concatenate(
            [
                jnp.concatenate([q[:, :HEAD_SIZE], one_hot], axis=1),
                jnp.concatenate([q[:, HEAD_SIZE:], one_hot], axis=1),
            ],
            axis=0,
        )
        return lax.dot_general(
            q, keys[part], (((1,), (1,)), ((), ())), preferred_element_type=jnp.float32
        )

    def weigh(scores):
        peak = jnp.max(scores, axis=1, keepdims=True)
        return jnp.exp2((scores - peak) * EXP2_SCALE).astype(jnp.bfloat16)

    def mix(weights, part, steps):
        mixed = jnp.dot(weights, vals[part], preferred_element_type=jnp.float32)
        result = (mixed[:, :HEAD_SIZE] / mixed[:, HEAD_SIZE:]).astype(jnp.bfloat16)
        result = jnp.concatenate([result[:TOK], result[TOK:]], axis=1)
        o_refs[steps][:, pl.ds(pl.multiple_of(part * PAIR, PAIR), PAIR)] = result

    for copy in copies:
        copy.wait()

    @pl.loop(0, parts)
    def _(part):
        scores = weights = None
        for steps in range(RING + 2):
            upcoming = score(part, steps) if steps < RING else None
            if weights is not None:
                mix(weights, part, steps - 2)
            weights = None if scores is None else weigh(scores)
            scores = upcoming


def attention(span_map, ctx, section, queries, units, chunk):
    smem = pl.BlockSpec(memory_space=pltpu.SMEM)
    vmem = pl.BlockSpec(memory_space=pltpu.VMEM)
    parts = PARTS[chunk]
    return pl.pallas_call(
        functools.partial(attention_kernel, chunk),
        in_specs=[smem, smem, smem, pl.BlockSpec(memory_space=pltpu.HBM)] + [vmem] * SPANS,
        out_specs=[vmem] * RING,
        out_shape=[jax.ShapeDtypeStruct((TOK, parts * PAIR), jnp.bfloat16)] * RING,
        scratch_shapes=[
            pltpu.VMEM((parts, TOK, GROUP * HEAD_SIZE), jnp.bfloat16),
            pltpu.VMEM((parts, TRACE, PAIR), jnp.bfloat16),
            pltpu.VMEM((parts, TRACE, PAIR), jnp.bfloat16),
            pltpu.SemaphoreType.DMA((parts,)),
        ],
        compiler_params=pltpu.CompilerParams(vmem_limit_bytes=VMEM_LIMIT),
        cost_estimate=pl.CostEstimate(
            flops=parts * GROUP * TOK * TRACE * PAIR * 2 * 2,
            bytes_accessed=parts * (TRACE * PAIR + GROUP * TOK * PAIR) * 2,
            transcendentals=parts * GROUP * TOK * TRACE,
        ),
        name="attention",
    )(pinned(span_map), ctx, section, pinned(queries), *units)


def total_kernel(a, b, c, d, o_ref):
    f32 = jnp.float32
    o_ref[...] = (
        a[...].astype(f32) + b[...].astype(f32) + (c[...].astype(f32) + d[...].astype(f32))
    ).astype(jnp.bfloat16)


def row_total(slabs):
    return pl.pallas_call(
        total_kernel,
        in_specs=[pl.BlockSpec(memory_space=pltpu.VMEM)] * RING,
        out_specs=pl.BlockSpec(memory_space=pltpu.VMEM),
        out_shape=jax.ShapeDtypeStruct(slabs[0].shape, jnp.bfloat16),
        compiler_params=pltpu.CompilerParams(vmem_limit_bytes=4 * 2**20),
        name="row_total",
    )(*slabs)


def prefix_kernel(chunk, section, residual_ref, *refs):
    slabs, below, outs = refs[:RING], refs[RING : 2 * RING - 1], refs[2 * RING - 1 : 3 * RING - 1]
    ordered, summed = refs[3 * RING - 1 :]
    place, row = section[0] % RING, section[0] // RING
    for steps in range(RING):
        ordered[(place + RING - steps) % RING] = slabs[steps][...]
    for part in range(PARTS[chunk]):
        columns = slice(part * PAIR, (part + 1) * PAIR)
        first = (BASES[chunk] + part) * GROUP * HEAD_SIZE + place * PAIR
        state = residual_ref[:, pl.ds(pl.multiple_of(first, PAIR), PAIR)].astype(jnp.float32)
        for steps, rows in enumerate(below, 1):
            earlier = rows[:, columns].astype(jnp.float32)
            state = state + jnp.where(row >= steps, earlier, 0.0)
        for layer in range(RING):
            state = state + ordered[layer, :, columns].astype(jnp.float32)
            summed[layer, :, columns] = state.astype(jnp.bfloat16)
    for steps in range(RING):
        outs[steps][...] = summed[(place + steps) % RING]


def prefix(section, residual, slabs, below, chunk):
    slab = jax.ShapeDtypeStruct(slabs[0].shape, jnp.bfloat16)
    whole = pl.BlockSpec(memory_space=pltpu.VMEM)
    return pl.pallas_call(
        functools.partial(prefix_kernel, chunk),
        in_specs=[pl.BlockSpec(memory_space=pltpu.SMEM)] + [whole] * (2 * RING),
        out_specs=[whole] * RING,
        out_shape=[slab] * RING,
        scratch_shapes=[
            pltpu.VMEM((RING, *slab.shape), jnp.bfloat16),
            pltpu.VMEM((RING, *slab.shape), jnp.bfloat16),
        ],
        compiler_params=pltpu.CompilerParams(vmem_limit_bytes=8 * 2**20),
        name="prefix",
    )(section, residual, *slabs, *below)


def assemble_kernel(section, *refs):
    slabs, o_ref = refs[:-1], refs[-1]
    place = section[0] % RING
    for chunk in range(CHUNKS):
        for steps in range(RING):
            column = (place + RING - steps) % RING * PAIR
            for part in range(PARTS[chunk]):
                first = (BASES[chunk] + part) * GROUP * HEAD_SIZE + column
                o_ref[0, :, pl.ds(pl.multiple_of(first, PAIR), PAIR)] = slabs[
                    chunk * RING + steps
                ][:, part * PAIR : (part + 1) * PAIR]


def assemble(section, slabs):
    whole = pl.BlockSpec(memory_space=pltpu.VMEM)
    width = KEY_VALUE_HEADS * GROUP * HEAD_SIZE
    return pl.pallas_call(
        assemble_kernel,
        in_specs=[pl.BlockSpec(memory_space=pltpu.SMEM)] + [whole] * len(slabs),
        out_specs=whole,
        out_shape=jax.ShapeDtypeStruct((1, TOK, width), jnp.bfloat16),
        compiler_params=pltpu.CompilerParams(vmem_limit_bytes=8 * 2**20),
        name="assemble",
    )(section, *slabs)


def turn(slabs):
    return [slabs[0]] + [
        lax.ppermute(slabs[steps], "section", turn_pairs(steps)) for steps in range(1, RING)
    ]


def body(queries, keys, values, residual, span_map):
    ctx = lax.axis_index("ctx")[None]
    section = lax.axis_index("section")[None]
    units = gather(keys, values)
    raw = [attention(span_map, ctx, section, queries[0], units, c) for c in range(CHUNKS)]
    slabs = [turn(r) for r in raw]
    slabs[0], _ = lax.optimization_barrier((slabs[0], raw[1]))
    finished, sums = [], None
    for chunk in range(CHUNKS):
        total = row_total(slabs[chunk])
        if sums is not None:
            total, *sums = lax.optimization_barrier((total, *sums))
            finished += turn(sums)
        below = [lax.ppermute(total, "section", climb_pairs(s)) for s in range(1, RING)]
        sums = prefix(section, residual, slabs[chunk], below, chunk)
    finished += turn(sums)
    return assemble(section, finished)


def solution(mesh):
    placed = (
        P("section", "ctx", None),
        P("section", "ctx", None),
        P("section", "ctx", None),
        P("ctx", None),
        P(),
    )
    return jax.shard_map(
        body, mesh=mesh, in_specs=placed, out_specs=P("section", "ctx", None), check_vma=False
    )
```

```python
import functools
import math

import jax
import jax.numpy as jnp
from jax import lax
from jax.experimental import pallas as pl
from jax.experimental.pallas import tpu as pltpu
from jax.sharding import PartitionSpec as P

KEY_VALUE_HEADS = 4
GROUP = 8
HEAD_SIZE = 128
TOK = 128
SPANS = 16
TRACE = SPANS * TOK
WIDTH = KEY_VALUE_HEADS * HEAD_SIZE
RING = 4
PAIR = 2 * HEAD_SIZE
EXP2_SCALE = math.log2(math.e) / math.sqrt(HEAD_SIZE)
HIDDEN = -1e30
VMEM_LIMIT = 24 * 2**20
CHUNKS = 2
PART = KEY_VALUE_HEADS // CHUNKS

SIDE = PART * HEAD_SIZE

UNITS = [(dx, dz, dc) for dc in range(2) for dz in range(2) for dx in range(4)]


def ctx_pairs(dx, dz, dc):
    pairs = []
    for i in range(SPANS):
        x, z, c = i // 4, i // 2 % 2, i % 2
        pairs.append((i, (x + dx) % 4 * 4 + (z ^ dz) * 2 + (c ^ dc)))
    return pairs


def ctx_move(unit, dx, dz, dc):
    return lax.ppermute(unit, "ctx", ctx_pairs(dx, dz, dc))


def turn_pairs(steps):
    return [(i, i // RING * RING + (i + steps) % RING) for i in range(RING * RING)]


def climb_pairs(steps):
    return [(i, (i + RING * steps) % (RING * RING)) for i in range(RING * RING)]


def pinned(x):
    return pltpu.with_memory_space_constraint(x, pltpu.HBM)


def join_kernel(k_ref, v_ref, o_ref, sems):
    copies = []
    for chunk in range(CHUNKS):
        for side, source in enumerate((k_ref, v_ref)):
            copies.append(
                pltpu.make_async_copy(
                    source.at[0, :, pl.ds(chunk * SIDE, SIDE)],
                    o_ref.at[:, pl.ds((2 * chunk + side) * SIDE, SIDE)],
                    sems.at[chunk, side],
                )
            )
    for copy in copies:
        copy.start()
    for copy in copies:
        copy.wait()


def join(keys, values):
    return pl.pallas_call(
        join_kernel,
        in_specs=[pl.BlockSpec(memory_space=pltpu.HBM)] * 2,
        out_specs=pl.BlockSpec(memory_space=pltpu.VMEM),
        out_shape=jax.ShapeDtypeStruct((TOK, 2 * WIDTH), jnp.bfloat16),
        scratch_shapes=[pltpu.SemaphoreType.DMA((CHUNKS, 2))],
        compiler_params=pltpu.CompilerParams(vmem_limit_bytes=2 * 2**20),
        name="join",
    )(pinned(keys), pinned(values))


def gather(keys, values):
    held = {(0, 0, 0): join(keys, values)}
    for dx, dz, source in (
        (0, 1, (0, 0, 0)),
        (1, 0, (0, 0, 0)),
        (3, 0, (0, 0, 0)),
        (0, 1, (1, 0, 0)),
        (1, 0, (1, 0, 0)),
        (3, 0, (0, 1, 0)),
        (0, 1, (2, 0, 0)),
    ):
        target = ((source[0] + dx) % 4, source[1] ^ dz, 0)
        held[target] = ctx_move(held[source], dx, dz, 0)
    for dz in range(2):
        for dx in range(4):
            held[dx, dz, 1] = ctx_move(held[dx, dz, 0], 0, 0, 1)
    return [held[unit] for unit in UNITS]


def attention_kernel(chunk, span_map, ctx, section, q_hbm, *refs):
    units, o_refs = refs[:SPANS], refs[SPANS : SPANS + RING]
    q_ref, keys, vals, sems = refs[SPANS + RING :]
    copies = []
    for part in range(PART):
        width = GROUP * HEAD_SIZE
        copies.append(
            pltpu.make_async_copy(
                q_hbm.at[:, pl.ds((chunk * PART + part) * width, width)],
                q_ref.at[part],
                sems.at[part],
            )
        )
        copies[-1].start()

    key_row = lax.broadcasted_iota(jnp.int32, (TOK, TOK), 0)
    query_row = lax.broadcasted_iota(jnp.int32, (TOK, TOK), 1)
    one_hot = jnp.where(key_row == query_row, 1.0, 0.0).astype(jnp.bfloat16)
    me = ctx[0]
    my_span = span_map[me]
    x, z, c = me // 4, me // 2 % 2, me % 2
    for block, (dx, dz, dc) in enumerate(UNITS):
        source = (x + 4 - dx) % 4 * 4 + (z + dz) % 2 * 2 + (c + dc) % 2
        ahead = (span_map[source] - my_span) * TOK + key_row - query_row
        mask = jnp.where(ahead > 0, HIDDEN, 0.0).astype(jnp.bfloat16)
        rows = slice(block * TOK, (block + 1) * TOK)
        for part in range(PART):
            first = chunk * 2 * SIDE + part * HEAD_SIZE
            keys[part, rows, :HEAD_SIZE] = units[block][:, first : first + HEAD_SIZE]
            keys[part, rows, HEAD_SIZE:] = mask
            first += SIDE
            vals[part, rows, :HEAD_SIZE] = units[block][:, first : first + HEAD_SIZE]
    for part in range(PART):
        vals[part, :, HEAD_SIZE:] = jnp.ones((TRACE, HEAD_SIZE), jnp.bfloat16)
    place = section[0] % RING

    def score(part, steps):
        first = pl.multiple_of((place + steps) % RING * PAIR, PAIR)
        q = q_ref[part, :, pl.ds(first, PAIR)]
        q = jnp.concatenate(
            [
                jnp.concatenate([q[:, :HEAD_SIZE], one_hot], axis=1),
                jnp.concatenate([q[:, HEAD_SIZE:], one_hot], axis=1),
            ],
            axis=0,
        )
        return lax.dot_general(
            q, keys[part], (((1,), (1,)), ((), ())), preferred_element_type=jnp.float32
        )

    def weigh(scores):
        peak = jnp.max(scores, axis=1, keepdims=True)
        return jnp.exp2((scores - peak) * EXP2_SCALE).astype(jnp.bfloat16)

    def mix(weights, part, steps):
        mixed = jnp.dot(weights, vals[part], preferred_element_type=jnp.float32)
        result = (mixed[:, :HEAD_SIZE] / mixed[:, HEAD_SIZE:]).astype(jnp.bfloat16)
        result = jnp.concatenate([result[:TOK], result[TOK:]], axis=1)
        o_refs[steps][:, pl.ds(pl.multiple_of(part * PAIR, PAIR), PAIR)] = result

    for copy in copies:
        copy.wait()

    @pl.loop(0, PART)
    def _(part):
        scores = weights = None
        for steps in range(RING + 2):
            upcoming = score(part, steps) if steps < RING else None
            if weights is not None:
                mix(weights, part, steps - 2)
            weights = None if scores is None else weigh(scores)
            scores = upcoming


def attention(span_map, ctx, section, queries, units, chunk):
    smem = pl.BlockSpec(memory_space=pltpu.SMEM)
    vmem = pl.BlockSpec(memory_space=pltpu.VMEM)
    return pl.pallas_call(
        functools.partial(attention_kernel, chunk),
        in_specs=[smem, smem, smem, pl.BlockSpec(memory_space=pltpu.HBM)] + [vmem] * SPANS,
        out_specs=[vmem] * RING,
        out_shape=[jax.ShapeDtypeStruct((TOK, PART * PAIR), jnp.bfloat16)] * RING,
        scratch_shapes=[
            pltpu.VMEM((PART, TOK, GROUP * HEAD_SIZE), jnp.bfloat16),
            pltpu.VMEM((PART, TRACE, PAIR), jnp.bfloat16),
            pltpu.VMEM((PART, TRACE, PAIR), jnp.bfloat16),
            pltpu.SemaphoreType.DMA((PART,)),
        ],
        compiler_params=pltpu.CompilerParams(vmem_limit_bytes=VMEM_LIMIT),
        cost_estimate=pl.CostEstimate(
            flops=PART * GROUP * TOK * TRACE * PAIR * 2 * 2,
            bytes_accessed=PART * (TRACE * PAIR + GROUP * TOK * PAIR) * 2,
            transcendentals=PART * GROUP * TOK * TRACE,
        ),
        name="attention",
    )(pinned(span_map), ctx, section, pinned(queries), *units)


def total_kernel(a, b, c, d, o_ref):
    f32 = jnp.float32
    o_ref[...] = (
        a[...].astype(f32) + b[...].astype(f32) + (c[...].astype(f32) + d[...].astype(f32))
    ).astype(jnp.bfloat16)


def row_total(slabs):
    return pl.pallas_call(
        total_kernel,
        in_specs=[pl.BlockSpec(memory_space=pltpu.VMEM)] * RING,
        out_specs=pl.BlockSpec(memory_space=pltpu.VMEM),
        out_shape=jax.ShapeDtypeStruct((TOK, PART * PAIR), jnp.bfloat16),
        compiler_params=pltpu.CompilerParams(vmem_limit_bytes=4 * 2**20),
        name="row_total",
    )(*slabs)


def prefix_kernel(chunk, section, residual_ref, *refs):
    slabs, below, outs = refs[:RING], refs[RING : 2 * RING - 1], refs[2 * RING - 1 : 3 * RING - 1]
    ordered, summed = refs[3 * RING - 1 :]
    place, row = section[0] % RING, section[0] // RING
    for steps in range(RING):
        ordered[(place + RING - steps) % RING] = slabs[steps][...]
    for part in range(PART):
        columns = slice(part * PAIR, (part + 1) * PAIR)
        first = (chunk * PART + part) * GROUP * HEAD_SIZE + place * PAIR
        state = residual_ref[:, pl.ds(pl.multiple_of(first, PAIR), PAIR)].astype(jnp.float32)
        for steps, rows in enumerate(below, 1):
            earlier = rows[:, columns].astype(jnp.float32)
            state = state + jnp.where(row >= steps, earlier, 0.0)
        for layer in range(RING):
            state = state + ordered[layer, :, columns].astype(jnp.float32)
            summed[layer, :, columns] = state.astype(jnp.bfloat16)
    for steps in range(RING):
        outs[steps][...] = summed[(place + steps) % RING]


def prefix(section, residual, slabs, below, chunk):
    slab = jax.ShapeDtypeStruct((TOK, PART * PAIR), jnp.bfloat16)
    whole = pl.BlockSpec(memory_space=pltpu.VMEM)
    return pl.pallas_call(
        functools.partial(prefix_kernel, chunk),
        in_specs=[pl.BlockSpec(memory_space=pltpu.SMEM)] + [whole] * (2 * RING),
        out_specs=[whole] * RING,
        out_shape=[slab] * RING,
        scratch_shapes=[
            pltpu.VMEM((RING, TOK, PART * PAIR), jnp.bfloat16),
            pltpu.VMEM((RING, TOK, PART * PAIR), jnp.bfloat16),
        ],
        compiler_params=pltpu.CompilerParams(vmem_limit_bytes=8 * 2**20),
        name="prefix",
    )(section, residual, *slabs, *below)


def assemble_kernel(section, *refs):
    slabs, o_ref = refs[:-1], refs[-1]
    place = section[0] % RING
    for chunk in range(CHUNKS):
        for steps in range(RING):
            column = (place + RING - steps) % RING * PAIR
            for part in range(PART):
                first = (chunk * PART + part) * GROUP * HEAD_SIZE + column
                o_ref[0, :, pl.ds(pl.multiple_of(first, PAIR), PAIR)] = slabs[
                    chunk * RING + steps
                ][:, part * PAIR : (part + 1) * PAIR]


def assemble(section, slabs):
    whole = pl.BlockSpec(memory_space=pltpu.VMEM)
    width = KEY_VALUE_HEADS * GROUP * HEAD_SIZE
    return pl.pallas_call(
        assemble_kernel,
        in_specs=[pl.BlockSpec(memory_space=pltpu.SMEM)] + [whole] * len(slabs),
        out_specs=whole,
        out_shape=jax.ShapeDtypeStruct((1, TOK, width), jnp.bfloat16),
        compiler_params=pltpu.CompilerParams(vmem_limit_bytes=8 * 2**20),
        name="assemble",
    )(section, *slabs)


def turn(slabs):
    return [slabs[0]] + [
        lax.ppermute(slabs[steps], "section", turn_pairs(steps)) for steps in range(1, RING)
    ]


def body(queries, keys, values, residual, span_map):
    ctx = lax.axis_index("ctx")[None]
    section = lax.axis_index("section")[None]
    units = gather(keys, values)
    raw = [attention(span_map, ctx, section, queries[0], units, c) for c in range(CHUNKS)]
    slabs = [turn(r) for r in raw]
    slabs[0], _ = lax.optimization_barrier((slabs[0], raw[1]))
    finished, sums = [], None
    for chunk in range(CHUNKS):
        total = row_total(slabs[chunk])
        if sums is not None:
            total, *sums = lax.optimization_barrier((total, *sums))
            finished += turn(sums)
        below = [lax.ppermute(total, "section", climb_pairs(s)) for s in range(1, RING)]
        sums = prefix(section, residual, slabs[chunk], below, chunk)
    finished += turn(sums)
    return assemble(section, finished)


def solution(mesh):
    placed = (
        P("section", "ctx", None),
        P("section", "ctx", None),
        P("section", "ctx", None),
        P("ctx", None),
        P(),
    )
    return jax.shard_map(
        body, mesh=mesh, in_specs=placed, out_specs=P("section", "ctx", None), check_vma=False
    )
```

```python
import functools
import math

import jax
import jax.numpy as jnp
from jax import lax
from jax.experimental import pallas as pl
from jax.experimental.pallas import tpu as pltpu
from jax.sharding import PartitionSpec as P

KEY_VALUE_HEADS = 4
GROUP = 8
HEAD_SIZE = 128
TOK = 128
SPANS = 16
TRACE = SPANS * TOK
WIDTH = KEY_VALUE_HEADS * HEAD_SIZE
RING = 4
OUTWARD = (0, 2, 1, 3)
PAIR = 2 * HEAD_SIZE
EXP2_SCALE = math.log2(math.e) / math.sqrt(HEAD_SIZE)
HIDDEN = -1e30
VMEM_LIMIT = 24 * 2**20
CHUNKS = 2
PART = KEY_VALUE_HEADS // CHUNKS

SIDE = PART * HEAD_SIZE

UNITS = [(dx, dz, dc) for dc in range(2) for dz in range(2) for dx in range(4)]


def ctx_pairs(dx, dz, dc):
    pairs = []
    for i in range(SPANS):
        x, z, c = i // 4, i // 2 % 2, i % 2
        pairs.append((i, (x + dx) % 4 * 4 + (z ^ dz) * 2 + (c ^ dc)))
    return pairs


def ctx_move(unit, dx, dz, dc):
    return lax.ppermute(unit, "ctx", ctx_pairs(dx, dz, dc))


def turn_pairs(steps):
    return [(i, i // RING * RING + (i + steps) % RING) for i in range(RING * RING)]


def climb_pairs(steps):
    return [(i, (i + RING * steps) % (RING * RING)) for i in range(RING * RING)]


def pinned(x):
    return pltpu.with_memory_space_constraint(x, pltpu.HBM)


def join_kernel(k_ref, v_ref, o_ref, sems):
    copies = []
    for chunk in range(CHUNKS):
        for side, source in enumerate((k_ref, v_ref)):
            copies.append(
                pltpu.make_async_copy(
                    source.at[0, :, pl.ds(chunk * SIDE, SIDE)],
                    o_ref.at[:, pl.ds((2 * chunk + side) * SIDE, SIDE)],
                    sems.at[chunk, side],
                )
            )
    for copy in copies:
        copy.start()
    for copy in copies:
        copy.wait()


def join(keys, values):
    return pl.pallas_call(
        join_kernel,
        in_specs=[pl.BlockSpec(memory_space=pltpu.HBM)] * 2,
        out_specs=pl.BlockSpec(memory_space=pltpu.VMEM),
        out_shape=jax.ShapeDtypeStruct((TOK, 2 * WIDTH), jnp.bfloat16),
        scratch_shapes=[pltpu.SemaphoreType.DMA((CHUNKS, 2))],
        compiler_params=pltpu.CompilerParams(vmem_limit_bytes=2 * 2**20),
        name="join",
    )(pinned(keys), pinned(values))


def gather(keys, values):
    held = {(0, 0, 0): join(keys, values)}
    for dx, dz, source in (
        (0, 1, (0, 0, 0)),
        (1, 0, (0, 0, 0)),
        (3, 0, (0, 0, 0)),
        (0, 1, (1, 0, 0)),
        (1, 0, (1, 0, 0)),
        (3, 0, (0, 1, 0)),
        (0, 1, (2, 0, 0)),
    ):
        target = ((source[0] + dx) % 4, source[1] ^ dz, 0)
        held[target] = ctx_move(held[source], dx, dz, 0)
    for dz in range(2):
        for dx in range(4):
            held[dx, dz, 1] = ctx_move(held[dx, dz, 0], 0, 0, 1)
    return [held[unit] for unit in UNITS]


def attention_kernel(chunk, span_map, ctx, section, q_hbm, *refs):
    units, o_refs = refs[:SPANS], refs[SPANS : SPANS + RING]
    q_ref, keys, vals, sems = refs[SPANS + RING :]
    copies = []
    for part in range(PART):
        width = GROUP * HEAD_SIZE
        copies.append(
            pltpu.make_async_copy(
                q_hbm.at[:, pl.ds((chunk * PART + part) * width, width)],
                q_ref.at[part],
                sems.at[part],
            )
        )
        copies[-1].start()

    key_row = lax.broadcasted_iota(jnp.int32, (TOK, TOK), 0)
    query_row = lax.broadcasted_iota(jnp.int32, (TOK, TOK), 1)
    one_hot = jnp.where(key_row == query_row, 1.0, 0.0).astype(jnp.bfloat16)
    me = ctx[0]
    my_span = span_map[me]
    x, z, c = me // 4, me // 2 % 2, me % 2
    for block, (dx, dz, dc) in enumerate(UNITS):
        source = (x + 4 - dx) % 4 * 4 + (z + dz) % 2 * 2 + (c + dc) % 2
        ahead = (span_map[source] - my_span) * TOK + key_row - query_row
        mask = jnp.where(ahead > 0, HIDDEN, 0.0).astype(jnp.bfloat16)
        rows = slice(block * TOK, (block + 1) * TOK)
        for part in range(PART):
            first = chunk * 2 * SIDE + part * HEAD_SIZE
            keys[part, rows, :HEAD_SIZE] = units[block][:, first : first + HEAD_SIZE]
            keys[part, rows, HEAD_SIZE:] = mask
            first += SIDE
            vals[part, rows, :HEAD_SIZE] = units[block][:, first : first + HEAD_SIZE]
    for part in range(PART):
        vals[part, :, HEAD_SIZE:] = jnp.ones((TRACE, HEAD_SIZE), jnp.bfloat16)
    place = section[0] % RING

    def score(part, steps):
        first = pl.multiple_of((place + steps) % RING * PAIR, PAIR)
        q = q_ref[part, :, pl.ds(first, PAIR)]
        q = jnp.concatenate(
            [
                jnp.concatenate([q[:, :HEAD_SIZE], one_hot], axis=1),
                jnp.concatenate([q[:, HEAD_SIZE:], one_hot], axis=1),
            ],
            axis=0,
        )
        return lax.dot_general(
            q, keys[part], (((1,), (1,)), ((), ())), preferred_element_type=jnp.float32
        )

    def weigh(scores):
        peak = jnp.max(scores, axis=1, keepdims=True)
        return jnp.exp2((scores - peak) * EXP2_SCALE).astype(jnp.bfloat16)

    def mix(weights, part, steps):
        mixed = jnp.dot(weights, vals[part], preferred_element_type=jnp.float32)
        result = (mixed[:, :HEAD_SIZE] / mixed[:, HEAD_SIZE:]).astype(jnp.bfloat16)
        result = jnp.concatenate([result[:TOK], result[TOK:]], axis=1)
        o_refs[steps][:, pl.ds(pl.multiple_of(part * PAIR, PAIR), PAIR)] = result

    for copy in copies:
        copy.wait()

    @pl.loop(0, PART)
    def _(part):
        scores = weights = None
        for steps in range(RING + 2):
            upcoming = score(part, steps) if steps < RING else None
            if weights is not None:
                mix(weights, part, steps - 2)
            weights = None if scores is None else weigh(scores)
            scores = upcoming


def attention(span_map, ctx, section, queries, units, chunk):
    smem = pl.BlockSpec(memory_space=pltpu.SMEM)
    vmem = pl.BlockSpec(memory_space=pltpu.VMEM)
    return pl.pallas_call(
        functools.partial(attention_kernel, chunk),
        in_specs=[smem, smem, smem, pl.BlockSpec(memory_space=pltpu.HBM)] + [vmem] * SPANS,
        out_specs=[vmem] * RING,
        out_shape=[jax.ShapeDtypeStruct((TOK, PART * PAIR), jnp.bfloat16)] * RING,
        scratch_shapes=[
            pltpu.VMEM((PART, TOK, GROUP * HEAD_SIZE), jnp.bfloat16),
            pltpu.VMEM((PART, TRACE, PAIR), jnp.bfloat16),
            pltpu.VMEM((PART, TRACE, PAIR), jnp.bfloat16),
            pltpu.SemaphoreType.DMA((PART,)),
        ],
        compiler_params=pltpu.CompilerParams(vmem_limit_bytes=VMEM_LIMIT),
        cost_estimate=pl.CostEstimate(
            flops=PART * GROUP * TOK * TRACE * PAIR * 2 * 2,
            bytes_accessed=PART * (TRACE * PAIR + GROUP * TOK * PAIR) * 2,
            transcendentals=PART * GROUP * TOK * TRACE,
        ),
        name="attention",
    )(pinned(span_map), ctx, section, pinned(queries), *units)


def total_kernel(a, b, c, d, o_ref):
    f32 = jnp.float32
    o_ref[...] = (
        a[...].astype(f32) + b[...].astype(f32) + (c[...].astype(f32) + d[...].astype(f32))
    ).astype(jnp.bfloat16)


def row_total(slabs):
    return pl.pallas_call(
        total_kernel,
        in_specs=[pl.BlockSpec(memory_space=pltpu.VMEM)] * RING,
        out_specs=pl.BlockSpec(memory_space=pltpu.VMEM),
        out_shape=jax.ShapeDtypeStruct((TOK, PART * PAIR), jnp.bfloat16),
        compiler_params=pltpu.CompilerParams(vmem_limit_bytes=4 * 2**20),
        name="row_total",
    )(*(slabs[steps] for steps in OUTWARD))


def prefix_kernel(chunk, section, residual_ref, *refs):
    slabs, below, outs = refs[:RING], refs[RING : 2 * RING - 1], refs[2 * RING - 1 : 3 * RING - 1]
    ordered, summed = refs[3 * RING - 1 :]
    place, row = section[0] % RING, section[0] // RING
    for steps in range(RING):
        ordered[(place + RING - steps) % RING] = slabs[OUTWARD.index(steps)][...]
    for part in range(PART):
        columns = slice(part * PAIR, (part + 1) * PAIR)
        first = (chunk * PART + part) * GROUP * HEAD_SIZE + place * PAIR
        state = residual_ref[:, pl.ds(pl.multiple_of(first, PAIR), PAIR)].astype(jnp.float32)
        for steps, rows in enumerate(below, 1):
            earlier = rows[:, columns].astype(jnp.float32)
            state = state + jnp.where(row >= steps, earlier, 0.0)
        for layer in range(RING):
            state = state + ordered[layer, :, columns].astype(jnp.float32)
            summed[layer, :, columns] = state.astype(jnp.bfloat16)
    for steps in range(RING):
        outs[steps][...] = summed[(place + steps) % RING]


def prefix(section, residual, slabs, below, chunk):
    slab = jax.ShapeDtypeStruct((TOK, PART * PAIR), jnp.bfloat16)
    whole = pl.BlockSpec(memory_space=pltpu.VMEM)
    return pl.pallas_call(
        functools.partial(prefix_kernel, chunk),
        in_specs=[pl.BlockSpec(memory_space=pltpu.SMEM)] + [whole] * (2 * RING),
        out_specs=[whole] * RING,
        out_shape=[slab] * RING,
        scratch_shapes=[
            pltpu.VMEM((RING, TOK, PART * PAIR), jnp.bfloat16),
            pltpu.VMEM((RING, TOK, PART * PAIR), jnp.bfloat16),
        ],
        compiler_params=pltpu.CompilerParams(vmem_limit_bytes=8 * 2**20),
        name="prefix",
    )(section, residual, *(slabs[steps] for steps in OUTWARD), *below)


def assemble_kernel(section, *refs):
    slabs, o_ref = refs[:-1], refs[-1]
    place = section[0] % RING
    for chunk in range(CHUNKS):
        for steps in range(RING):
            column = (place + RING - OUTWARD[steps]) % RING * PAIR
            for part in range(PART):
                first = (chunk * PART + part) * GROUP * HEAD_SIZE + column
                o_ref[0, :, pl.ds(pl.multiple_of(first, PAIR), PAIR)] = slabs[
                    chunk * RING + steps
                ][:, part * PAIR : (part + 1) * PAIR]


def assemble(section, slabs):
    whole = pl.BlockSpec(memory_space=pltpu.VMEM)
    width = KEY_VALUE_HEADS * GROUP * HEAD_SIZE
    return pl.pallas_call(
        assemble_kernel,
        in_specs=[pl.BlockSpec(memory_space=pltpu.SMEM)] + [whole] * len(slabs),
        out_specs=whole,
        out_shape=jax.ShapeDtypeStruct((1, TOK, width), jnp.bfloat16),
        compiler_params=pltpu.CompilerParams(vmem_limit_bytes=8 * 2**20),
        name="assemble",
    )(section, *(slabs[c * RING + steps] for c in range(CHUNKS) for steps in OUTWARD))


def turn(slabs):
    return [slabs[0]] + [
        lax.ppermute(slabs[steps], "section", turn_pairs(steps)) for steps in range(1, RING)
    ]


def body(queries, keys, values, residual, span_map):
    ctx = lax.axis_index("ctx")[None]
    section = lax.axis_index("section")[None]
    units = gather(keys, values)
    raw = [attention(span_map, ctx, section, queries[0], units, c) for c in range(CHUNKS)]
    slabs = [turn(r) for r in raw]
    slabs[0], _ = lax.optimization_barrier((slabs[0], raw[1]))
    finished, sums = [], None
    for chunk in range(CHUNKS):
        total = row_total(slabs[chunk])
        if sums is not None:
            total, *sums = lax.optimization_barrier((total, *sums))
            finished += turn(sums)
        below = [lax.ppermute(total, "section", climb_pairs(s)) for s in range(1, RING)]
        sums = prefix(section, residual, slabs[chunk], below, chunk)
    finished += turn(sums)
    return assemble(section, finished)


def solution(mesh):
    placed = (
        P("section", "ctx", None),
        P("section", "ctx", None),
        P("section", "ctx", None),
        P("ctx", None),
        P(),
    )
    return jax.shard_map(
        body, mesh=mesh, in_specs=placed, out_specs=P("section", "ctx", None), check_vma=False
    )
```
